512 devices in a mesh: blk: 64 (over z_lo, y, x), merge: 8 (over z_hi, core).
Axes of the slice: x: 4, y: 4, z: 16 (z_hi: 4, z_lo: 4; z = z_hi * 4 + z_lo), core: 2. Of those that a mesh axis runs over, the one named last changes fastest.
Arguments:
- series: float32 [524288], P(('blk', 'merge')), may hold values from -6 to 6
- tail: float32 [63], replicated, may hold values from -6 to 6
- excl: int32 [1], replicated, may hold values from 64 to 4095
- band: int32 [1], replicated, may hold values from 12288 to 16383
Outputs:
- profile: float32 [524288], P(('blk', 'merge'))
The draws below stay inside these ranges and needn't reach their ends.
All inputs are finite; a program needn't handle non-finite values.
Results may differ from the reference program's by a relative error of at most 0.0003.
Values sent between devices are 32-bit elements; how exact they have to be, the bound alone decides.
A program may use at most 128 MiB of HBM per device.

```python
import jax
import jax.numpy as jnp
from jax import lax

M = 64
R = 8192
STEPS = 2
NW = 524288
N_BLK = 64


def level_of(stream_key, shape, shards, smallest, top_value):
    def one(axis_at, parts):
        steps = jax.random.uniform(jax.random.fold_in(jax.random.fold_in(stream_key, 6), axis_at), (parts,), jnp.float32, smallest / len(shards), top_value / len(shards))
        return jnp.repeat(jnp.exp(steps), shape[axis_at] // parts).reshape((-1,) + (1,) * (len(shape) - axis_at - 1))

    loudness = one(*shards[0])
    for cut in shards[1:]:
        loudness = loudness * one(*cut)
    return loudness


def gaussian(rng, shape, scale, bound, pieces=(), kind=jnp.bfloat16):
    entries = scale * jax.random.normal(rng, shape, jnp.float32)
    if pieces:
        entries = entries * level_of(rng, shape, pieces, -0.22, 0.18)
    return jnp.clip(entries, -bound, bound).astype(kind)


def setup_inputs(seed: int = 0) -> dict:
    splits = jax.random.split(jax.random.key(seed), 5)
    series = gaussian(splits[0], (NW,), 1.0, 6.0, ((0, 512),), jnp.float32)
    tail = gaussian(splits[1], (M - 1,), 1.0, 6.0, (), jnp.float32)
    excl = jax.random.randint(splits[2], (1,), M, R // 2).astype(jnp.int32)
    band = jax.random.randint(splits[3], (1,), (STEPS - 1) * R + R // 2, STEPS * R).astype(jnp.int32)
    return dict(series=series, tail=tail, excl=excl, band=band)


BIG = 4.0

def normalize(ext, count, width):
    windows = jnp.stack([lax.slice_in_dim(ext, k, k + count) for k in range(width)], 0)
    mean = lax.optimization_barrier(jnp.mean(windows, 0))
    cent = windows - mean
    var = lax.optimization_barrier(jnp.mean(cent * cent, 0))
    return cent * lax.rsqrt(var + 1e-06)

def reference(series, tail, excl, band):
    total = series.shape[0]
    width = tail.shape[0] + 1
    ext = jnp.concatenate([series, tail])
    normed = normalize(ext, total, width)
    padded = jnp.concatenate([normed, jnp.zeros((width, STEPS * R), jnp.float32)], 1)
    offs = jnp.arange(R, dtype=jnp.int32)

    def one_block(colmin, blk_id):
        start = (blk_id * R).astype(jnp.int32)
        rows = lax.dynamic_slice(normed, (jnp.int32(0), start), (width, R))
        row_index = start + offs
        rowmin = jnp.full((R,), BIG, jnp.float32)
        for step in range(STEPS):
            cstart = (start + step * R).astype(jnp.int32)
            cols = lax.dynamic_slice(padded, (jnp.int32(0), cstart), (width, R))
            corr = lax.dot_general(rows, cols, (((0,), (0,)), ((), ())), precision=lax.Precision.HIGHEST, preferred_element_type=jnp.float32)
            value = 1.0 - corr * (1.0 / width)
            col_index = cstart + offs
            diag = col_index[None, :] - row_index[:, None]
            keep = (diag > excl[0]) & (diag <= band[0]) & (col_index[None, :] < total)
            value = jnp.where(keep, value, BIG)
            rowmin = jnp.minimum(rowmin, lax.optimization_barrier(jnp.min(value, 1)))
            seg = lax.dynamic_slice_in_dim(colmin, cstart, R)
            colmin = lax.dynamic_update_slice_in_dim(colmin, jnp.minimum(seg, lax.optimization_barrier(jnp.min(value, 0))), cstart, 0)
        return (colmin, rowmin)
    colmin0 = jnp.full((total + STEPS * R,), BIG, jnp.float32)
    colmin, rowmins = lax.scan(one_block, colmin0, jnp.arange(N_BLK, dtype=jnp.int32))
    return jnp.minimum(rowmins.reshape(total), colmin[:total])
```

```python
import functools

import jax
import jax.numpy as jnp
from jax import lax
from jax.experimental import pallas as pl
from jax.experimental.pallas import tpu as pltpu
from jax.sharding import PartitionSpec as P

LOW = -192.0
LANES = 128
SUBS = 8
MESH = pl.DeviceIdType.MESH


def normal_windows(line, count, width):
    length = line.shape[1]
    rows = jnp.broadcast_to(line, (SUBS, length))
    parts = [
        pltpu.roll(rows, length - (width - 1) + first, 1, stride=1, stride_axis=0)[:, :count]
        for first in range(0, width, SUBS)
    ]
    mean = jnp.sum(functools.reduce(jnp.add, parts), 0, keepdims=True) * (1.0 / width)
    cent = [part - mean for part in parts]
    squares = functools.reduce(jnp.add, [part * part for part in cent])
    var = jnp.sum(squares, 0, keepdims=True) * (1.0 / width)
    inv = lax.rsqrt(var + 1e-06)
    return jnp.concatenate([part * inv for part in cent], 0)


def halves(z):
    high = z.astype(jnp.bfloat16)
    low = (z - high.astype(jnp.float32)).astype(jnp.bfloat16)
    return high, low


def put_columns(ref, z):
    high, low = halves(z)
    width = z.shape[0]
    for at, part in enumerate((high, low, high, low)):
        ref[at * width : (at + 1) * width, :] = part


def put_rows(ref, z):
    high, low = halves(jnp.transpose(z))
    width = z.shape[0]
    ref[:, : 2 * width] = jnp.concatenate([high, high], 1)
    ref[:, 2 * width :] = jnp.concatenate([low, low], 1)


def tile(rows_ref, cols_ref, best_ref, limit_ref, base, with_columns):
    count = rows_ref.shape[0]
    step = min(256, count)
    tops = []
    for first in range(0, count, step):
        corr = jnp.dot(
            rows_ref[...], cols_ref[:, first : first + step], preferred_element_type=jnp.float32
        )
        best = None
        for lane in range(first, first + step, LANES):
            part = corr[:, lane - first : lane - first + LANES].reshape(count // SUBS, SUBS, LANES)
            limit = limit_ref[pl.ds(base - lane // SUBS, count // SUBS)]
            part = jnp.minimum(part, limit)
            if with_columns:
                tops.append(jnp.max(part, 0))
            best = part if best is None else jnp.maximum(best, part)
        best_ref[...] = jnp.maximum(best_ref[...], best.reshape(count, LANES))
    if with_columns:
        return jnp.max(jnp.concatenate(tops, 1), 0, keepdims=True)


def kernel(
    blocks, groups, width,
    series_ref, tail_ref, excl_ref, band_ref, out_ref,
    x_ref, rows_ref, own_ref, even_ref, odd_ref, best_ref, limit_ref, cols_ref, got_ref,
    send_sem, recv_sem, back_send_sem, back_recv_sem,
):
    count = series_ref.shape[1]
    unit = count // SUBS
    half = groups // 2
    blk = lax.axis_index("blk")
    grp = lax.axis_index("merge")
    rim = half + 1
    nxt = half + 2
    after = nxt + groups
    last = after + 1

    def device(d_blk, d_grp):
        return (lax.rem(blk + d_blk + blocks, blocks), lax.rem(grp + d_grp + groups, groups))

    barrier = pltpu.get_barrier_semaphore()
    sources = [device(0, t) for t in range(1, rim + 1)]
    sources += [device(1, u) for u in range(groups)]
    sources += [(lax.rem(blk + 2, blocks), 0)]
    for source in sources:
        pl.semaphore_signal(barrier, inc=1, device_id=source, device_id_type=MESH)

    x_ref[0] = series_ref[...]
    x_ref[last, :, : width - 1] = tail_ref[...]
    best_ref[...] = jnp.full(best_ref.shape, LOW, jnp.float32)

    far = 18 * unit
    base_half = far + unit
    base_own = far + 3 * unit
    excl = excl_ref[0]
    band = band_ref[0]
    skew = lax.broadcasted_iota(jnp.int32, (16, SUBS, LANES), 2)
    skew = skew - lax.broadcasted_iota(jnp.int32, (16, SUBS, LANES), 1)
    skew = skew - SUBS * lax.broadcasted_iota(jnp.int32, (16, SUBS, LANES), 0)
    sign = jnp.where(grp + half >= groups, -1, 1)

    def fill(start, stop, base, keep):
        def body(i, _):
            at = start + i * 16
            diff = skew + SUBS * (base - at)
            limit_ref[pl.ds(at, 16)] = jnp.where(keep(diff), -LOW, LOW)
            return 0

        lax.fori_loop(0, (stop - start) // 16, body, 0)

    fill(0, far, far, lambda d: (d > excl) & (d <= band))

    pl.semaphore_wait(barrier, rim + groups + jnp.where(grp == 0, groups, 0))

    def sending(src, dst, slot, target):
        return pltpu.make_async_remote_copy(
            src_ref=src, dst_ref=dst, send_sem=send_sem.at[slot], recv_sem=recv_sem.at[slot],
            device_id=target, device_id_type=MESH,
        )

    head = series_ref.at[:, :LANES]
    copies = [sending(series_ref, x_ref.at[t], t, device(0, -t)) for t in range(1, half + 1)]
    copies += [sending(head, x_ref.at[rim, :, :LANES], rim, device(0, -rim))]
    copies += [
        sending(series_ref, x_ref.at[nxt + u], nxt + u, device(-1, -u)) for u in range(groups)
    ]
    for copy in copies:
        copy.start()
    behind = lax.rem(blk + blocks - 2, blocks)

    def head_copy(u):
        return pltpu.make_async_remote_copy(
            src_ref=head, dst_ref=x_ref.at[after, :, :LANES], send_sem=send_sem.at[last + u],
            recv_sem=recv_sem.at[after], device_id=(behind, u), device_id_type=MESH,
        )

    @pl.when(grp == 0)
    def _():
        for u in range(groups):
            head_copy(u).start()

    fill(far, far + 2 * unit, base_half, lambda d: half * count + sign * d > excl)
    fill(far + 2 * unit, far + 4 * unit, base_own, lambda d: jnp.abs(d) > excl)

    for copy in copies:
        copy.wait()
    head_copy(0).wait_recv()

    @pl.when(grp == 0)
    def _():
        for u in range(groups):
            head_copy(u).wait_send()

    def windows_of_block(t):
        ends = lax.rem(grp + t, groups) == groups - 1
        over = jnp.where(blk == blocks - 1, last, nxt + lax.rem(groups - grp, groups))
        return t, jnp.where(ends, over, t + 1)

    def windows_of_next(u):
        ends = lax.rem(grp + u, groups) == groups - 1
        over = jnp.where(blk == blocks - 2, last, after)
        return nxt + u, jnp.where(ends, over, nxt + lax.rem(u + 1, groups))

    def windows(slot, rest):
        line = jnp.concatenate([x_ref[slot], x_ref[rest, :, :LANES]], 1)
        return normal_windows(line, count, width)

    near = half - 1
    pieces = near + groups

    def place(k):
        t_slot, t_rest = windows_of_block(k + 1)
        u_slot, u_rest = windows_of_next(k - near)
        inside = k < near
        return jnp.where(inside, t_slot, u_slot), jnp.where(inside, t_rest, u_rest)

    def base_of(k):
        wraps = grp + k + 1 >= groups
        t_off = jnp.where(wraps, groups, k + 1)
        u_off = groups + lax.rem(grp + k - near + groups, groups) - grp
        u_off = jnp.where(blk == blocks - 1, 17, u_off)
        return far - unit * jnp.where(k < near, t_off, u_off)

    def back(k):
        inside = k < near
        d_blk = jnp.where(inside, 0, 1)
        d_grp = jnp.where(inside, k + 1, k - near)
        return pltpu.make_async_remote_copy(
            src_ref=cols_ref.at[k], dst_ref=got_ref.at[k], send_sem=back_send_sem.at[k],
            recv_sem=back_recv_sem.at[k], device_id=device(d_blk, d_grp), device_id_type=MESH,
        )

    z = windows(*windows_of_block(0))
    put_rows(rows_ref, z)
    put_columns(own_ref, z)
    put_columns(even_ref, windows(*place(0)))

    def meet(k, now_ref):
        cols_ref[k] = tile(rows_ref, now_ref, best_ref, limit_ref, base_of(k), True)
        back(k).start()

    def pair(i, _):
        k = 2 * i
        put_columns(odd_ref, windows(*place(k + 1)))
        meet(k, even_ref)
        put_columns(even_ref, windows(*place(k + 2)))
        meet(k + 1, odd_ref)
        return 0

    lax.fori_loop(0, (pieces - 1) // 2, pair, 0)
    put_columns(odd_ref, windows(*windows_of_block(half)))
    meet(pieces - 1, even_ref)
    tile(rows_ref, odd_ref, best_ref, limit_ref, base_half, False)
    tile(rows_ref, own_ref, best_ref, limit_ref, base_own, False)
    top = jnp.max(jnp.transpose(best_ref[...]), 0, keepdims=True)
    for k in range(pieces):
        back(k).wait()
        top = jnp.maximum(top, got_ref[k])
    out_ref[...] = 1.0 - top * (1.0 / width)


def on_device(blocks, groups, series, tail, excl, band):
    count = series.shape[0]
    width = tail.shape[0] + 1
    half = groups // 2
    pieces = half - 1 + groups
    slots = half + 2 + groups + 2
    vmem = pl.BlockSpec(memory_space=pltpu.VMEM)
    smem = pl.BlockSpec(memory_space=pltpu.SMEM)
    window_cols = pltpu.VMEM((4 * width, count), jnp.bfloat16)
    out = pl.pallas_call(
        functools.partial(kernel, blocks, groups, width),
        out_shape=jax.ShapeDtypeStruct((1, count), jnp.float32),
        in_specs=[vmem, vmem, smem, smem],
        out_specs=vmem,
        scratch_shapes=[
            pltpu.VMEM((slots, 1, count), jnp.float32),
            pltpu.VMEM((count, 4 * width), jnp.bfloat16),
            window_cols,
            window_cols,
            window_cols,
            pltpu.VMEM((count, LANES), jnp.float32),
            pltpu.VMEM((22 * count // SUBS, SUBS, LANES), jnp.float32),
            pltpu.VMEM((pieces, 1, count), jnp.float32),
            pltpu.VMEM((pieces, 1, count), jnp.float32),
            pltpu.SemaphoreType.DMA((slots - 1 + groups,)),
            pltpu.SemaphoreType.DMA((slots - 1,)),
            pltpu.SemaphoreType.DMA((pieces,)),
            pltpu.SemaphoreType.DMA((pieces,)),
        ],
        compiler_params=pltpu.CompilerParams(
            collective_id=0, has_side_effects=True, vmem_limit_bytes=40 * 1024 * 1024
        ),
    )(series.reshape(1, count), tail.reshape(1, width - 1), excl, band)
    return out.reshape(count)


def solution(mesh):
    placed = (P(("blk", "merge")), P(), P(), P())
    body = functools.partial(on_device, mesh.shape["blk"], mesh.shape["merge"])
    return jax.shard_map(
        body, mesh=mesh, in_specs=placed, out_specs=P(("blk", "merge")), check_vma=False
    )
```

```python
import functools

import jax
import jax.numpy as jnp
from jax import lax
from jax.experimental import pallas as pl
from jax.experimental.pallas import tpu as pltpu
from jax.sharding import PartitionSpec as P

LOW = -192.0
LANES = 128
SUBS = 8
MESH = pl.DeviceIdType.MESH


def normal_windows(line, count, width):
    length = line.shape[1]
    rows = jnp.broadcast_to(line, (SUBS, length))
    parts = [
        pltpu.roll(rows, length - (width - 1) + first, 1, stride=1, stride_axis=0)[:, :count]
        for first in range(0, width, SUBS)
    ]
    mean = jnp.sum(functools.reduce(jnp.add, parts), 0, keepdims=True) * (1.0 / width)
    cent = [part - mean for part in parts]
    squares = functools.reduce(jnp.add, [part * part for part in cent])
    var = jnp.sum(squares, 0, keepdims=True) * (1.0 / width)
    inv = lax.rsqrt(var + 1e-06)
    return jnp.concatenate([part * inv for part in cent], 0)


def halves(z):
    high = z.astype(jnp.bfloat16)
    low = (z - high.astype(jnp.float32)).astype(jnp.bfloat16)
    return high, low


def put_columns(ref, z):
    high, low = halves(z)
    width = z.shape[0]
    for at, part in enumerate((high, low, high, low)):
        ref[at * width : (at + 1) * width, :] = part


def put_rows(ref, z):
    high, low = halves(jnp.transpose(z))
    width = z.shape[0]
    ref[:, : 2 * width] = jnp.concatenate([high, high], 1)
    ref[:, 2 * width :] = jnp.concatenate([low, low], 1)


def tile(rows_ref, cols_ref, best_ref, limit_ref, row, base):
    count = cols_ref.shape[1]
    mine = pl.ds(row * count, count)
    step = min(256, count)
    tops = []
    for first in range(0, count, step):
        corr = jnp.dot(
            rows_ref[mine, :], cols_ref[:, first : first + step], preferred_element_type=jnp.float32
        )
        best = None
        for lane in range(first, first + step, LANES):
            part = corr[:, lane - first : lane - first + LANES].reshape(count // SUBS, SUBS, LANES)
            limit = limit_ref[pl.ds(base - lane // SUBS, count // SUBS)]
            part = jnp.minimum(part, limit)
            tops.append(jnp.max(part, 0))
            best = part if best is None else jnp.maximum(best, part)
        best_ref[mine, :] = jnp.maximum(best_ref[mine, :], best.reshape(count, LANES))
    return jnp.max(jnp.concatenate(tops, 1), 0, keepdims=True)


def pick(k, entries):
    out = entries[-1]
    for at in range(len(entries) - 2, -1, -1):
        out = jnp.where(k == at, entries[at], out)
    return out


SPREAD = ((0, 1, 2), (0, -1, 1), (0, 2, 3), (-1, 0, 4), (-1, -1, 5), (-1, 1, 6), (-1, 2, 7), (1, 2, 8))
PLACE = ((0, 0), (0, 1), (0, -1), (0, 2), (1, 0), (1, 1), (1, -1), (1, 2), (-1, 2))
PAIRED = 9


def kernel(
    blocks, groups, width,
    series_hbm, tail_hbm, excl_hbm, band_hbm, out_ref,
    own_ref, short_ref, tail_ref, excl_ref, band_ref, x_ref, rows_ref, even_ref, odd_ref, best_ref, limit_ref,
    cols_ref, got_ref, local_sem, send_sem, recv_sem, head_sem, back_send_sem, back_recv_sem, ready_sem,
):
    count = own_ref.shape[1]
    unit = count // SUBS
    planes = groups // 2
    blk = lax.axis_index("blk")
    grp = lax.axis_index("merge")
    plane = lax.div(grp, 2)
    core = lax.rem(grp, 2)

    def at_plane(d_plane):
        return lax.rem(plane + d_plane + 2 * planes, planes)

    def device(d_blk, d_plane, c):
        return (lax.rem(blk + d_blk + 2 * blocks, blocks), at_plane(d_plane) * 2 + c)

    sibling = device(0, 0, 1 - core)
    loads = [
        pltpu.make_async_copy(series_hbm, own_ref, local_sem.at[0]),
        pltpu.make_async_copy(tail_hbm, short_ref, local_sem.at[1]),
        pltpu.make_async_copy(excl_hbm, excl_ref, local_sem.at[2]),
        pltpu.make_async_copy(band_hbm, band_ref, local_sem.at[3]),
    ]
    for load in loads:
        load.start()

    barrier = pltpu.get_barrier_semaphore()

    def greet(target):
        pl.semaphore_signal(barrier, inc=1, device_id=target, device_id_type=MESH)

    for d_blk in (0, 1, -1):
        greet(device(d_blk, 2, 0))
    greet(sibling)
    for d_blk, d_plane in ((0, 1), (0, -1), (1, 0), (1, 1), (1, -1)):
        greet(device(d_blk, d_plane, 1))

    @pl.when(core == 1)
    def _():
        greet((lax.rem(blk + 2, blocks), jnp.where(plane == 2, 0, 1)))

        @pl.when(plane != 1)
        def _():
            greet(device(-1, -1, 1))

    loads[0].wait()
    x_ref[0, :, :count] = own_ref[...]
    first_plane = plane == 0
    far_count = 7 + jnp.where(first_plane, 1, 0)
    near_count = 11 + jnp.where(first_plane, 3, 1)
    pl.semaphore_wait(barrier, jnp.where(core == 0, far_count, near_count))
    pl.semaphore_signal(ready_sem, inc=1, device_id=sibling, device_id_type=MESH)

    def send_piece(slot, target):
        return pltpu.make_async_remote_copy(
            src_ref=own_ref, dst_ref=x_ref.at[slot, :, :count], send_sem=send_sem.at[slot],
            recv_sem=recv_sem.at[slot], device_id=target, device_id_type=MESH,
        )

    def send_head(slot, at, target):
        return pltpu.make_async_remote_copy(
            src_ref=own_ref.at[:, :LANES], dst_ref=x_ref.at[slot, :, count:], send_sem=send_sem.at[10 + at],
            recv_sem=head_sem.at[0 if at in (0, 9) else at], device_id=target, device_id_type=MESH,
        )

    back_blk = jnp.where(first_plane, -1, 0)
    pieces = {slot: send_piece(slot, device(d, dp, core)) for d, dp, slot in SPREAD}
    pieces[PAIRED] = send_piece(PAIRED, sibling)
    heads_odd = {slot: send_head(slot, slot, device(d, dp, 0)) for d, dp, slot in SPREAD}
    heads_even = {slot: send_head(slot, slot, device(back_blk + d, dp - 1, 1)) for d, dp, slot in SPREAD}
    heads_even[0] = send_head(0, 0, device(back_blk, -1, 1))
    heads_even[9] = send_head(PAIRED, 9, device(back_blk, -1, 0))

    @pl.when(core == 0)
    def _():
        for slot in (3, 7, 8):
            pieces[slot].start()
        for slot in (1, 5):
            heads_even[slot].start()
        pl.semaphore_wait(ready_sem, 1)
        pieces[PAIRED].start()
        for slot in (0, 9, 2, 3, 4, 6, 7, 8):
            heads_even[slot].start()
        for slot in (1, 2, 5, 6, 4):
            pieces[slot].start()

    @pl.when(core == 1)
    def _():
        pieces[PAIRED].start()
        for slot in (1, 2, 5, 6, 4):
            pieces[slot].start()
        for slot in (1, 2, 5, 6, 4):
            heads_odd[slot].start()
        pl.semaphore_wait(ready_sem, 1)
        for slot in (3, 7, 8):
            pieces[slot].start()
        for slot in (3, 7, 8):
            heads_odd[slot].start()

    for load in loads[1:]:
        load.wait()
    tail_ref[...] = jnp.zeros(tail_ref.shape, jnp.float32)
    tail_ref[:, : width - 1] = short_ref[...]
    best_ref[...] = jnp.full(best_ref.shape, LOW, jnp.float32)

    far = 18 * unit
    base_own = 37 * unit
    total = 38 * unit
    excl = excl_ref[0]
    band = band_ref[0]
    skew = lax.broadcasted_iota(jnp.int32, (16, SUBS, LANES), 2)
    skew = skew - lax.broadcasted_iota(jnp.int32, (16, SUBS, LANES), 1)
    skew = skew - SUBS * lax.broadcasted_iota(jnp.int32, (16, SUBS, LANES), 0)

    def fill(start, stop, diff_of, keep):
        def body(i, _):
            at = start + i * 16
            limit_ref[pl.ds(at, 16)] = jnp.where(keep(diff_of(at)), -LOW, LOW)
            return 0

        lax.fori_loop(0, (stop - start) // 16, body, 0)

    inside = lambda d: (d > excl) & (d <= band)
    fill(0, far, lambda at: skew + SUBS * (far - at), inside)
    fill(far, 2 * far, lambda at: SUBS * (at - far) - skew, inside)
    fill(2 * far, total, lambda at: skew + SUBS * (base_own - at), lambda d: jnp.abs(d) > excl)

    def base_of(slot, row):
        d_blk, d_plane = PLACE[slot]
        g = at_plane(d_plane) * 2 + core
        mine = plane * 2 + row
        if d_blk == 0:
            step = g - mine
            return jnp.where(step == 0, base_own, far - unit * step)
        if d_blk == 1:
            return far - unit * jnp.where(blk == blocks - 1, 17, groups + g - mine)
        return far + unit * jnp.where(blk == 0, 17, groups + mine - g)

    def is_last(d_blk, d_plane, c):
        return (blk + d_blk == blocks - 1) & (at_plane(d_plane) == planes - 1) & (c == 1)

    def windows(slot, over):
        line = x_ref[slot]
        rest = jnp.where(over, tail_ref[...], line[:, count:])
        return normal_windows(jnp.concatenate([line[:, :count], rest], 1), count, width)

    def piece_windows(slot, over):
        @pl.when(slot != 0)
        def _():
            pieces_in(slot).wait_recv()
            head_in(slot).wait_recv()

        return windows(slot, over)

    def pieces_in(slot):
        return pltpu.make_async_remote_copy(
            src_ref=own_ref, dst_ref=x_ref.at[slot, :, :count], send_sem=send_sem.at[0],
            recv_sem=recv_sem.at[slot], device_id=sibling, device_id_type=MESH,
        )

    def head_in(slot):
        return pltpu.make_async_remote_copy(
            src_ref=own_ref.at[:, :LANES], dst_ref=x_ref.at[slot, :, count:], send_sem=send_sem.at[0],
            recv_sem=head_sem.at[slot], device_id=sibling, device_id_type=MESH,
        )

    pieces_in(PAIRED).wait_recv()

    @pl.when(core == 0)
    def _():
        x_ref[0, :, count:] = x_ref[PAIRED, :, :LANES]
        pltpu.make_async_remote_copy(
            src_ref=own_ref.at[:, :LANES], dst_ref=x_ref.at[PAIRED, :, count:], send_sem=send_sem.at[0],
            recv_sem=head_sem.at[0], device_id=sibling, device_id_type=MESH,
        ).wait_recv()

    @pl.when(core == 1)
    def _():
        x_ref[PAIRED, :, count:] = own_ref[:, :LANES]
        head_in(0).wait_recv()

    for row in range(2):
        slot = jnp.where(core == row, 0, PAIRED)
        put_rows(rows_ref.at[pl.ds(row * count, count)], windows(slot, is_last(0, 0, row)))

    order = (2, 1, 6, 5, 4, 0, 3, 7, 8)
    returns = {2: 3, 1: 4, 6: 1, 5: 2, 4: 0}
    singles = (1 - core, core)
    last_list = [is_last(*PLACE[slot], core) for slot in order]
    base_lists = [[base_of(slot, row) for slot in order] for row in range(2)]
    back_list = [returns.get(slot, -1) for slot in order]
    step_list = [PLACE[slot][0] for slot in order]
    plane_list = [PLACE[slot][1] for slot in order]

    def build(k, ref):
        put_columns(ref, piece_windows(pick(k, order), pick(k, last_list)))

    def back(k, slot, target):
        return pltpu.make_async_remote_copy(
            src_ref=cols_ref.at[k], dst_ref=got_ref.at[slot], send_sem=back_send_sem.at[k],
            recv_sem=back_recv_sem.at[slot], device_id=target, device_id_type=MESH,
        )

    def give_back(k):
        slot = pick(k, back_list)

        @pl.when(slot >= 0)
        def _():
            back(k, slot, device(pick(k, step_list), pick(k, plane_list), core)).start()

    def meet_one(k, now_ref, row):
        base = jnp.where(row == 0, base_lists[0][k], base_lists[1][k])
        cols_ref[k] = tile(rows_ref, now_ref, best_ref, limit_ref, row, base)
        give_back(k)

    def meet(k, now_ref):
        tops = [
            tile(rows_ref, now_ref, best_ref, limit_ref, row, pick(k, base_lists[row]))
            for row in range(2)
        ]
        cols_ref[k] = jnp.maximum(*tops)
        give_back(k)

    build(0, even_ref)
    build(1, odd_ref)
    meet_one(0, even_ref, singles[0])
    build(2, even_ref)
    meet_one(1, odd_ref, singles[1])

    def pair(i, _):
        k = 2 * i + 2
        build(k + 1, odd_ref)
        meet(k, even_ref)
        build(k + 2, even_ref)
        meet(k + 1, odd_ref)
        return 0

    lax.fori_loop(0, 3, pair, 0)
    meet(8, even_ref)

    def row_tops(row):
        return jnp.max(jnp.transpose(best_ref[pl.ds(row * count, count), :]), 0, keepdims=True)

    cols_ref[9] = row_tops(1 - core)
    back(9, 5, sibling).start()
    top = jnp.maximum(row_tops(core), cols_ref[order.index(0)])
    for slot in range(1, 10):
        pieces[slot].wait_send()

    @pl.when(core == 0)
    def _():
        for copy in heads_even.values():
            copy.wait_send()

    @pl.when(core == 1)
    def _():
        for copy in heads_odd.values():
            copy.wait_send()

    for slot, k in enumerate((4, 2, 3, 0, 1, 9)):
        back(k, slot, sibling).wait()
        top = jnp.maximum(top, got_ref[slot])
    out_ref[...] = 1.0 - top * (1.0 / width)


def on_device(blocks, groups, series, tail, excl, band):
    count = series.shape[0]
    width = tail.shape[0] + 1
    hbm = pl.BlockSpec(memory_space=pltpu.HBM)
    window_cols = pltpu.VMEM((4 * width, count), jnp.bfloat16)
    out = pl.pallas_call(
        functools.partial(kernel, blocks, groups, width),
        out_shape=jax.ShapeDtypeStruct((1, count), jnp.float32),
        in_specs=[hbm, hbm, hbm, hbm],
        out_specs=pl.BlockSpec(memory_space=pltpu.VMEM),
        scratch_shapes=[
            pltpu.VMEM((1, count), jnp.float32),
            pltpu.VMEM((1, width - 1), jnp.float32),
            pltpu.VMEM((1, LANES), jnp.float32),
            pltpu.SMEM((1,), jnp.int32),
            pltpu.SMEM((1,), jnp.int32),
            pltpu.VMEM((10, 1, count + LANES), jnp.float32),
            pltpu.VMEM((2 * count, 4 * width), jnp.bfloat16),
            window_cols,
            window_cols,
            pltpu.VMEM((2 * count, LANES), jnp.float32),
            pltpu.VMEM((38 * count // SUBS, SUBS, LANES), jnp.float32),
            pltpu.VMEM((10, 1, count), jnp.float32),
            pltpu.VMEM((6, 1, count), jnp.float32),
            pltpu.SemaphoreType.DMA((4,)),
            pltpu.SemaphoreType.DMA((20,)),
            pltpu.SemaphoreType.DMA((10,)),
            pltpu.SemaphoreType.DMA((10,)),
            pltpu.SemaphoreType.DMA((10,)),
            pltpu.SemaphoreType.DMA((6,)),
            pltpu.SemaphoreType.REGULAR,
        ],
        compiler_params=pltpu.CompilerParams(
            collective_id=0, has_side_effects=True, vmem_limit_bytes=48 * 1024 * 1024
        ),
    )(series.reshape(1, count), tail.reshape(1, width - 1), excl, band)
    return out.reshape(count)


def solution(mesh):
    placed = (P(("blk", "merge")), P(), P(), P())
    body = functools.partial(on_device, mesh.shape["blk"], mesh.shape["merge"])
    return jax.shard_map(
        body, mesh=mesh, in_specs=placed, out_specs=P(("blk", "merge")), check_vma=False
    )
```

```python
import functools

import jax
import jax.numpy as jnp
from jax import lax
from jax.experimental import pallas as pl
from jax.experimental.pallas import tpu as pltpu
from jax.sharding import PartitionSpec as P

LOW = -192.0
LANES = 128
SUBS = 8
MESH = pl.DeviceIdType.MESH


def normal_windows(line, count, width):
    length = line.shape[1]
    rows = jnp.broadcast_to(line, (SUBS, length))
    parts = [
        pltpu.roll(rows, length - (width - 1) + first, 1, stride=1, stride_axis=0)[:, :count]
        for first in range(0, width, SUBS)
    ]
    mean = jnp.sum(functools.reduce(jnp.add, parts), 0, keepdims=True) * (1.0 / width)
    cent = [part - mean for part in parts]
    squares = functools.reduce(jnp.add, [part * part for part in cent])
    var = jnp.sum(squares, 0, keepdims=True) * (1.0 / width)
    inv = lax.rsqrt(var + 1e-06)
    return jnp.concatenate([part * inv for part in cent], 0)


def halves(z):
    high = z.astype(jnp.bfloat16)
    low = (z - high.astype(jnp.float32)).astype(jnp.bfloat16)
    return high, low


def put_columns(ref, z):
    high, low = halves(z)
    width = z.shape[0]
    for at, part in enumerate((high, low, high, low)):
        ref[at * width : (at + 1) * width, :] = part


def put_rows(ref, z):
    high, low = halves(jnp.transpose(z))
    width = z.shape[0]
    ref[:, : 2 * width] = jnp.concatenate([high, high], 1)
    ref[:, 2 * width :] = jnp.concatenate([low, low], 1)


def tile(rows_ref, cols_ref, best_ref, limit_ref, row, base):
    count = cols_ref.shape[1]
    mine = pl.ds(row * count, count)
    step = min(256, count)
    tops = []
    for first in range(0, count, step):
        corr = jnp.dot(
            rows_ref[mine, :], cols_ref[:, first : first + step], preferred_element_type=jnp.float32
        )
        best = None
        for lane in range(first, first + step, LANES):
            part = corr[:, lane - first : lane - first + LANES].reshape(count // SUBS, SUBS, LANES)
            limit = limit_ref[pl.ds(base - lane // SUBS, count // SUBS)]
            part = jnp.minimum(part, limit)
            tops.append(jnp.max(part, 0))
            best = part if best is None else jnp.maximum(best, part)
        best_ref[mine, :] = jnp.maximum(best_ref[mine, :], best.reshape(count, LANES))
    return jnp.max(jnp.concatenate(tops, 1), 0, keepdims=True)


def pick(k, entries):
    out = entries[-1]
    for at in range(len(entries) - 2, -1, -1):
        out = jnp.where(k == at, entries[at], out)
    return out


SPREAD = ((0, 1, 2), (0, -1, 1), (0, 2, 3), (-1, 0, 4), (-1, -1, 5), (-1, 1, 6), (-1, 2, 7), (1, 2, 8))
PLACE = ((0, 0), (0, 1), (0, -1), (0, 2), (1, 0), (1, 1), (1, -1), (1, 2), (-1, 2))
PAIRED = 9


def kernel(
    blocks, groups, width,
    series_hbm, tail_hbm, excl_hbm, band_hbm, out_ref,
    own_ref, short_ref, tail_ref, excl_ref, band_ref, x_ref, rows_ref, even_ref, odd_ref, best_ref, limit_ref,
    cols_ref, got_ref, local_sem, send_sem, recv_sem, head_sem, back_send_sem, back_recv_sem, ready_sem, far_sem,
):
    count = own_ref.shape[1]
    unit = count // SUBS
    planes = groups // 2
    blk = lax.axis_index("blk")
    grp = lax.axis_index("merge")
    plane = lax.div(grp, 2)
    core = lax.rem(grp, 2)

    def at_plane(d_plane):
        return lax.rem(plane + d_plane + 2 * planes, planes)

    def device(d_blk, d_plane, c):
        return (lax.rem(blk + d_blk + 2 * blocks, blocks), at_plane(d_plane) * 2 + c)

    sibling = device(0, 0, 1 - core)
    loads = [
        pltpu.make_async_copy(series_hbm, own_ref, local_sem.at[0]),
        pltpu.make_async_copy(tail_hbm, short_ref, local_sem.at[1]),
        pltpu.make_async_copy(excl_hbm, excl_ref, local_sem.at[2]),
        pltpu.make_async_copy(band_hbm, band_ref, local_sem.at[3]),
    ]
    for load in loads:
        load.start()

    barrier = pltpu.get_barrier_semaphore()

    def greet(target):
        pl.semaphore_signal(barrier, inc=1, device_id=target, device_id_type=MESH)

    ahead = plane < 2

    @pl.when(ahead)
    def _():
        for d_blk in (0, 1, -1):
            greet(device(d_blk, 2, 0))

    greet(sibling)
    for d_blk, d_plane in ((0, 1), (0, -1), (1, 0), (1, 1), (1, -1)):
        greet(device(d_blk, d_plane, 1))

    @pl.when(core == 1)
    def _():
        @pl.when(plane != 2)
        def _():
            greet((lax.rem(blk + 2, blocks), 1))

        @pl.when(plane != 1)
        def _():
            greet(device(-1, -1, 1))

    far = 18 * unit
    base_own = 37 * unit
    total = 38 * unit

    def fill_bounds():
        excl = excl_ref[0]
        band = band_ref[0]
        skew = lax.broadcasted_iota(jnp.int32, (16, SUBS, LANES), 2)
        skew = skew - lax.broadcasted_iota(jnp.int32, (16, SUBS, LANES), 1)
        skew = skew - SUBS * lax.broadcasted_iota(jnp.int32, (16, SUBS, LANES), 0)

        def fill(start, stop, diff_of, keep):
            def body(i, _):
                at = start + i * 16
                limit_ref[pl.ds(at, 16)] = jnp.where(keep(diff_of(at)), -LOW, LOW)
                return 0

            lax.fori_loop(0, (stop - start) // 16, body, 0)

        inside = lambda d: (d > excl) & (d <= band)
        fill(0, far, lambda at: skew + SUBS * (far - at), inside)
        fill(far, 2 * far, lambda at: SUBS * (at - far) - skew, inside)
        fill(2 * far, total, lambda at: skew + SUBS * (base_own - at), lambda d: jnp.abs(d) > excl)

    for load in loads:
        load.wait()
    x_ref[0, :, :count] = own_ref[...]

    @pl.when(ahead)
    def _():
        fill_bounds()

    first_plane = plane == 0
    far_count = jnp.where(ahead, 1, 7)
    near_count = 11 + jnp.where(first_plane, 3, 1)
    pl.semaphore_wait(barrier, jnp.where(core == 0, far_count, near_count))

    def tell(sem, target):
        pl.semaphore_signal(sem, inc=1, device_id=target, device_id_type=MESH)

    behind = jnp.logical_not(ahead)

    @pl.when((core == 1) | behind)
    def _():
        tell(ready_sem, sibling)

    @pl.when((core == 0) & behind)
    def _():
        for d_blk in (0, 1, -1):
            tell(far_sem, device(d_blk, 2, 0))


    def send_piece(slot, target):
        return pltpu.make_async_remote_copy(
            src_ref=own_ref, dst_ref=x_ref.at[slot, :, :count], send_sem=send_sem.at[slot],
            recv_sem=recv_sem.at[slot], device_id=target, device_id_type=MESH,
        )

    def send_head(slot, at, target):
        return pltpu.make_async_remote_copy(
            src_ref=own_ref.at[:, :LANES], dst_ref=x_ref.at[slot, :, count:], send_sem=send_sem.at[10 + at],
            recv_sem=head_sem.at[0 if at in (0, 9) else at], device_id=target, device_id_type=MESH,
        )

    back_blk = jnp.where(first_plane, -1, 0)
    pieces = {slot: send_piece(slot, device(d, dp, core)) for d, dp, slot in SPREAD}
    pieces[PAIRED] = send_piece(PAIRED, sibling)
    heads_odd = {slot: send_head(slot, slot, device(d, dp, 0)) for d, dp, slot in SPREAD}
    heads_even = {
        slot: send_head(slot, slot, device(back_blk + d, dp - 1, 1)) for d, dp, slot in SPREAD if dp != -1
    }
    heads_even[0] = send_head(0, 0, device(back_blk, -1, 1))
    heads_even[9] = send_head(PAIRED, 9, device(back_blk, -1, 0))

    def far_even():
        for slot in (3, 7, 8):
            pieces[slot].start()

    def near_even():
        pl.semaphore_wait(ready_sem, 1)
        for slot in (0, 9):
            heads_even[slot].start()
        pieces[PAIRED].start()
        for slot in (2, 6):
            pieces[slot].start()
            heads_even[slot].start()
        for slot in (4, 5, 1):
            pieces[slot].start()
        for slot in (4, 3, 7, 8):
            heads_even[slot].start()

    @pl.when((core == 0) & behind)
    def _():
        far_even()
        near_even()

    @pl.when((core == 0) & ahead)
    def _():
        near_even()
        pl.semaphore_wait(far_sem, 3)
        tell(ready_sem, sibling)
        far_even()

    @pl.when(core == 1)
    def _():
        pieces[PAIRED].start()
        for slot in (2, 6, 4, 5, 1):
            pieces[slot].start()
            heads_odd[slot].start()
        pl.semaphore_wait(ready_sem, 1)
        for slot in (3, 7, 8):
            pieces[slot].start()
        for slot in (3, 7, 8):
            heads_odd[slot].start()

    tail_ref[...] = jnp.zeros(tail_ref.shape, jnp.float32)
    tail_ref[:, : width - 1] = short_ref[...]
    best_ref[...] = jnp.full(best_ref.shape, LOW, jnp.float32)

    @pl.when(behind)
    def _():
        fill_bounds()

    def base_of(slot, row):
        d_blk, d_plane = PLACE[slot]
        g = at_plane(d_plane) * 2 + core
        mine = plane * 2 + row
        if d_blk == 0:
            step = g - mine
            return jnp.where(step == 0, base_own, far - unit * step)
        if d_blk == 1:
            return far - unit * jnp.where(blk == blocks - 1, 17, groups + g - mine)
        return far + unit * jnp.where(blk == 0, 17, groups + mine - g)

    def is_last(d_blk, d_plane, c):
        return (blk + d_blk == blocks - 1) & (at_plane(d_plane) == planes - 1) & (c == 1)

    def windows(slot, over):
        line = x_ref[slot]
        rest = jnp.where(over, tail_ref[...], line[:, count:])
        return normal_windows(jnp.concatenate([line[:, :count], rest], 1), count, width)

    def pieces_in(slot):
        return pltpu.make_async_remote_copy(
            src_ref=own_ref, dst_ref=x_ref.at[slot, :, :count], send_sem=send_sem.at[0],
            recv_sem=recv_sem.at[slot], device_id=sibling, device_id_type=MESH,
        )

    def head_in(slot):
        return pltpu.make_async_remote_copy(
            src_ref=own_ref.at[:, :LANES], dst_ref=x_ref.at[slot, :, count:], send_sem=send_sem.at[0],
            recv_sem=head_sem.at[slot], device_id=sibling, device_id_type=MESH,
        )

    relays = [
        pltpu.make_async_remote_copy(
            src_ref=x_ref.at[0, :, count:], dst_ref=x_ref.at[slot, :, count:], send_sem=send_sem.at[20 + at],
            recv_sem=head_sem.at[slot], device_id=device(-at, -1, 1), device_id_type=MESH,
        )
        for at, slot in enumerate((1, 5))
    ]

    pieces_in(PAIRED).wait_recv()

    @pl.when(core == 0)
    def _():
        x_ref[0, :, count:] = x_ref[PAIRED, :, :LANES]
        pltpu.make_async_remote_copy(
            src_ref=own_ref.at[:, :LANES], dst_ref=x_ref.at[PAIRED, :, count:], send_sem=send_sem.at[0],
            recv_sem=head_sem.at[0], device_id=sibling, device_id_type=MESH,
        ).wait_recv()

    @pl.when(core == 1)
    def _():
        x_ref[PAIRED, :, count:] = own_ref[:, :LANES]
        head_in(0).wait_recv()
        for copy in relays:
            copy.start()

    for row in range(2):
        slot = jnp.where(core == row, 0, PAIRED)
        put_rows(rows_ref.at[pl.ds(row * count, count)], windows(slot, is_last(0, 0, row)))

    slots = len(PLACE)
    last_plane = plane == planes - 1
    shared = (jnp.where(last_plane, 1, 2), jnp.where(last_plane, 2, 1))
    common = (4, 0, 3, 7, 8)
    order = [
        jnp.where(first_plane, at_first, jnp.where(last_plane, at_last, between))
        for at_first, at_last, between in zip((6, 4, 0, 5) + common[2:], (5, 6) + common, (6, 5) + common)
    ]
    last_list = [is_last(*PLACE[slot], core) for slot in range(slots)]
    base_lists = [[base_of(slot, row) for slot in range(slots)] for row in range(2)]
    step_list = [PLACE[slot][0] for slot in range(slots)]
    plane_list = [PLACE[slot][1] for slot in range(slots)]
    back_list = [-1, 4, 3, -1, 0, 2, 1, -1, -1]

    def build(slot, ref):
        put_columns(ref, windows(slot, pick(slot, last_list)))

    def arrive(slot):
        @pl.when(slot != 0)
        def _():
            pieces_in(slot).wait_recv()
            head_in(slot).wait_recv()

    def back(slot, at, target):
        return pltpu.make_async_remote_copy(
            src_ref=cols_ref.at[slot], dst_ref=got_ref.at[at], send_sem=back_send_sem.at[slot],
            recv_sem=back_recv_sem.at[at], device_id=target, device_id_type=MESH,
        )

    def give_back(slot):
        back(slot, pick(slot, back_list), device(pick(slot, step_list), pick(slot, plane_list), core)).start()

    def meet_shared(slot, now_ref):
        one = jnp.where(slot == 2, 1 - core, core)
        whole = plane == jnp.where(slot == 2, 1, planes - 1)
        low = jnp.where(whole, 0, one)
        high = jnp.where(whole, 2, jnp.where(first_plane, one, one + 1))
        cols_ref[slot] = jnp.full((1, count), LOW, jnp.float32)

        def body(at, _):
            base = jnp.where(at == 0, pick(slot, base_lists[0]), pick(slot, base_lists[1]))
            top = tile(rows_ref, now_ref, best_ref, limit_ref, at, base)
            cols_ref[slot] = jnp.maximum(cols_ref[slot], top)
            return 0

        lax.fori_loop(low, high, body, 0)

        @pl.when(plane != 0)
        def _():
            give_back(slot)

    def meet(slot, now_ref):
        tops = [
            tile(rows_ref, now_ref, best_ref, limit_ref, row, pick(slot, base_lists[row]))
            for row in range(2)
        ]
        cols_ref[slot] = jnp.maximum(*tops)

        @pl.when(pick(slot, back_list) >= 0)
        def _():
            give_back(slot)

    @pl.when(plane != 0)
    def _():
        arrive(shared[0])
        build(shared[0], even_ref)

    meet_shared(shared[0], even_ref)
    arrive(order[0])
    build(order[0], odd_ref)

    @pl.when(plane != 0)
    def _():
        arrive(shared[1])
        build(shared[1], even_ref)

    meet_shared(shared[1], even_ref)

    def pair(i, _):
        k = 2 * i
        now, then, after = (pick(k + at, order) for at in range(3))
        arrive(then)
        build(then, even_ref)
        meet(now, odd_ref)
        arrive(after)
        build(after, odd_ref)
        meet(then, even_ref)
        return 0

    lax.fori_loop(0, 3, pair, 0)
    meet(order[6], odd_ref)

    @pl.when(plane == 0)
    def _():
        for slot in (1, 2):
            arrive(slot)

    def row_tops(row):
        return jnp.max(jnp.transpose(best_ref[pl.ds(row * count, count), :]), 0, keepdims=True)

    cols_ref[9] = row_tops(1 - core)
    back(9, 5, sibling).start()
    top = jnp.maximum(row_tops(core), cols_ref[0])
    for slot in range(1, 10):
        pieces[slot].wait_send()

    @pl.when(core == 0)
    def _():
        for copy in heads_even.values():
            copy.wait_send()

    @pl.when(core == 1)
    def _():
        for copy in list(heads_odd.values()) + relays:
            copy.wait_send()

    for slot in (4, 5, 6, 9):
        back(slot, 0, sibling).wait_send()

    @pl.when(plane != 0)
    def _():
        for slot in (1, 2):
            back(slot, 0, sibling).wait_send()

    for slot, silent in ((3, planes - 1), (4, 1)):

        @pl.when(plane == silent)
        def _():
            got_ref[slot] = jnp.full((1, count), LOW, jnp.float32)

        @pl.when(plane != silent)
        def _():
            back(0, slot, sibling).wait_recv()

    for slot in (0, 1, 2, 5):
        back(0, slot, sibling).wait_recv()
    for slot in range(6):
        top = jnp.maximum(top, got_ref[slot])
    out_ref[...] = 1.0 - top * (1.0 / width)


def on_device(blocks, groups, series, tail, excl, band):
    count = series.shape[0]
    width = tail.shape[0] + 1
    hbm = pl.BlockSpec(memory_space=pltpu.HBM)
    window_cols = pltpu.VMEM((4 * width, count), jnp.bfloat16)
    out = pl.pallas_call(
        functools.partial(kernel, blocks, groups, width),
        out_shape=jax.ShapeDtypeStruct((1, count), jnp.float32),
        in_specs=[hbm, hbm, hbm, hbm],
        out_specs=pl.BlockSpec(memory_space=pltpu.VMEM),
        scratch_shapes=[
            pltpu.VMEM((1, count), jnp.float32),
            pltpu.VMEM((1, width - 1), jnp.float32),
            pltpu.VMEM((1, LANES), jnp.float32),
            pltpu.SMEM((1,), jnp.int32),
            pltpu.SMEM((1,), jnp.int32),
            pltpu.VMEM((10, 1, count + LANES), jnp.float32),
            pltpu.VMEM((2 * count, 4 * width), jnp.bfloat16),
            window_cols,
            window_cols,
            pltpu.VMEM((2 * count, LANES), jnp.float32),
            pltpu.VMEM((38 * count // SUBS, SUBS, LANES), jnp.float32),
            pltpu.VMEM((10, 1, count), jnp.float32),
            pltpu.VMEM((6, 1, count), jnp.float32),
            pltpu.SemaphoreType.DMA((4,)),
            pltpu.SemaphoreType.DMA((22,)),
            pltpu.SemaphoreType.DMA((10,)),
            pltpu.SemaphoreType.DMA((10,)),
            pltpu.SemaphoreType.DMA((10,)),
            pltpu.SemaphoreType.DMA((6,)),
            pltpu.SemaphoreType.REGULAR,
            pltpu.SemaphoreType.REGULAR,
        ],
        compiler_params=pltpu.CompilerParams(
            collective_id=0, has_side_effects=True, vmem_limit_bytes=48 * 1024 * 1024
        ),
    )(series.reshape(1, count), pltpu.with_memory_space_constraint(tail.reshape(1, width - 1), pltpu.HBM), excl, band)
    return out.reshape(count)


def solution(mesh):
    placed = (P(("blk", "merge")), P(), P(), P())
    body = functools.partial(on_device, mesh.shape["blk"], mesh.shape["merge"])
    return jax.shard_map(
        body, mesh=mesh, in_specs=placed, out_specs=P(("blk", "merge")), check_vma=False
    )
```

```python
import functools

import jax
import jax.numpy as jnp
from jax import lax
from jax.experimental import pallas as pl
from jax.experimental.pallas import tpu as pltpu
from jax.sharding import PartitionSpec as P

LOW = -192.0
LANES = 128
SUBS = 8
MESH = pl.DeviceIdType.MESH


def normal_windows(line, count, width):
    length = line.shape[1]
    rows = jnp.broadcast_to(line, (SUBS, length))
    parts = [
        pltpu.roll(rows, length - (width - 1) + first, 1, stride=1, stride_axis=0)[:, :count]
        for first in range(0, width, SUBS)
    ]
    mean = jnp.sum(functools.reduce(jnp.add, parts), 0, keepdims=True) * (1.0 / width)
    cent = [part - mean for part in parts]
    squares = functools.reduce(jnp.add, [part * part for part in cent])
    var = jnp.sum(squares, 0, keepdims=True) * (1.0 / width)
    inv = lax.rsqrt(var + 1e-06)
    return jnp.concatenate([part * inv for part in cent], 0)


def halves(z):
    high = z.astype(jnp.bfloat16)
    low = (z - high.astype(jnp.float32)).astype(jnp.bfloat16)
    return high, low


def put_columns(ref, z):
    high, low = halves(z)
    width = z.shape[0]
    for at, part in enumerate((high, low, high, low)):
        ref[at * width : (at + 1) * width, :] = part


def put_rows(ref, z):
    high, low = halves(jnp.transpose(z))
    width = z.shape[0]
    ref[:, : 2 * width] = jnp.concatenate([high, high], 1)
    ref[:, 2 * width :] = jnp.concatenate([low, low], 1)


def tile(rows_ref, cols_ref, best_ref, limit_ref, row, base):
    count = cols_ref.shape[1]
    mine = pl.ds(row * count, count)
    step = min(256, count)
    tops = []
    for first in range(0, count, step):
        corr = jnp.dot(
            rows_ref[mine, :], cols_ref[:, first : first + step], preferred_element_type=jnp.float32
        )
        best = None
        for lane in range(first, first + step, LANES):
            part = corr[:, lane - first : lane - first + LANES].reshape(count // SUBS, SUBS, LANES)
            limit = limit_ref[pl.ds(base - lane // SUBS, count // SUBS)]
            part = jnp.minimum(part, limit)
            tops.append(jnp.max(part, 0))
            best = part if best is None else jnp.maximum(best, part)
        best_ref[mine, :] = jnp.maximum(best_ref[mine, :], best.reshape(count, LANES))
    return jnp.max(jnp.concatenate(tops, 1), 0, keepdims=True)


def pick(k, entries):
    out = entries[-1]
    for at in range(len(entries) - 2, -1, -1):
        out = jnp.where(k == at, entries[at], out)
    return out


SPREAD = ((0, 1, 2), (0, -1, 1), (0, 2, 3), (-1, 0, 4), (-1, -1, 5), (-1, 1, 6), (-1, 2, 7), (1, 2, 8))
PLACE = ((0, 0), (0, 1), (0, -1), (0, 2), (1, 0), (1, 1), (1, -1), (1, 2), (-1, 2))
PAIRED = 9


def kernel(
    blocks, groups, width,
    series_hbm, tail_hbm, excl_hbm, band_hbm, out_ref,
    own_ref, short_ref, tail_ref, excl_ref, band_ref, x_ref, rows_ref, even_ref, odd_ref, best_ref, limit_ref,
    cols_ref, got_ref, local_sem, send_sem, recv_sem, head_sem, back_send_sem, back_recv_sem, ready_sem, far_sem,
):
    count = own_ref.shape[1]
    unit = count // SUBS
    planes = groups // 2
    blk = lax.axis_index("blk")
    grp = lax.axis_index("merge")
    plane = lax.div(grp, 2)
    core = lax.rem(grp, 2)

    def at_plane(d_plane):
        return lax.rem(plane + d_plane + 2 * planes, planes)

    def device(d_blk, d_plane, c):
        return (lax.rem(blk + d_blk + 2 * blocks, blocks), at_plane(d_plane) * 2 + c)

    sibling = device(0, 0, 1 - core)
    loads = [
        pltpu.make_async_copy(series_hbm, own_ref, local_sem.at[0]),
        pltpu.make_async_copy(tail_hbm, short_ref, local_sem.at[1]),
        pltpu.make_async_copy(excl_hbm, excl_ref, local_sem.at[2]),
        pltpu.make_async_copy(band_hbm, band_ref, local_sem.at[3]),
    ]
    for load in loads:
        load.start()

    barrier = pltpu.get_barrier_semaphore()

    def greet(target):
        pl.semaphore_signal(barrier, inc=1, device_id=target, device_id_type=MESH)

    ahead = plane < 2

    @pl.when(ahead)
    def _():
        for d_blk in (0, 1, -1):
            greet(device(d_blk, 2, 0))

    greet(sibling)
    for d_blk, d_plane in ((0, 1), (0, -1), (1, 0), (1, 1), (1, -1)):
        greet(device(d_blk, d_plane, 1))

    @pl.when(core == 1)
    def _():
        @pl.when(plane != 2)
        def _():
            greet((lax.rem(blk + 2, blocks), 1))

        @pl.when(plane != 1)
        def _():
            greet(device(-1, -1, 1))

    far = 18 * unit
    base_own = 37 * unit
    total = 38 * unit

    def fill_bounds():
        excl = excl_ref[0]
        band = band_ref[0]
        skew = lax.broadcasted_iota(jnp.int32, (16, SUBS, LANES), 2)
        skew = skew - lax.broadcasted_iota(jnp.int32, (16, SUBS, LANES), 1)
        skew = skew - SUBS * lax.broadcasted_iota(jnp.int32, (16, SUBS, LANES), 0)

        def fill(start, stop, diff_of, keep):
            def body(i, _):
                at = start + i * 16
                limit_ref[pl.ds(at, 16)] = jnp.where(keep(diff_of(at)), -LOW, LOW)
                return 0

            lax.fori_loop(0, (stop - start) // 16, body, 0)

        inside = lambda d: (d > excl) & (d <= band)
        fill(0, far, lambda at: skew + SUBS * (far - at), inside)
        fill(far, 2 * far, lambda at: SUBS * (at - far) - skew, inside)
        fill(2 * far, total, lambda at: skew + SUBS * (base_own - at), lambda d: jnp.abs(d) > excl)

    for load in loads:
        load.wait()
    x_ref[0, :, :count] = own_ref[...]

    @pl.when(ahead)
    def _():
        fill_bounds()

    first_plane = plane == 0
    far_count = jnp.where(ahead, 1, 7)
    near_count = 11 + jnp.where(first_plane, 3, 1)
    pl.semaphore_wait(barrier, jnp.where(core == 0, far_count, near_count))

    def tell(sem, target):
        pl.semaphore_signal(sem, inc=1, device_id=target, device_id_type=MESH)

    behind = jnp.logical_not(ahead)

    @pl.when((core == 1) | behind)
    def _():
        tell(ready_sem, sibling)

    @pl.when((core == 0) & behind)
    def _():
        for d_blk in (0, 1, -1):
            tell(far_sem, device(d_blk, 2, 0))


    def send_piece(slot, target):
        return pltpu.make_async_remote_copy(
            src_ref=own_ref, dst_ref=x_ref.at[slot, :, :count], send_sem=send_sem.at[slot],
            recv_sem=recv_sem.at[slot], device_id=target, device_id_type=MESH,
        )

    def send_head(slot, at, target):
        return pltpu.make_async_remote_copy(
            src_ref=own_ref.at[:, :LANES], dst_ref=x_ref.at[slot, :, count:], send_sem=send_sem.at[10 + at],
            recv_sem=head_sem.at[0 if at in (0, 9) else at], device_id=target, device_id_type=MESH,
        )

    back_blk = jnp.where(first_plane, -1, 0)
    pieces = {slot: send_piece(slot, device(d, dp, core)) for d, dp, slot in SPREAD}
    pieces[PAIRED] = send_piece(PAIRED, sibling)
    heads_odd = {slot: send_head(slot, slot, device(d, dp, 0)) for d, dp, slot in SPREAD}
    heads_even = {
        slot: send_head(slot, slot, device(back_blk + d, dp - 1, 1)) for d, dp, slot in SPREAD if dp != -1
    }
    heads_even[0] = send_head(0, 0, device(back_blk, -1, 1))
    heads_even[9] = send_head(PAIRED, 9, device(back_blk, -1, 0))

    def far_even():
        for slot in (3, 7, 8):
            pieces[slot].start()

    def near_even():
        pl.semaphore_wait(ready_sem, 1)
        for slot in (0, 9):
            heads_even[slot].start()
        pieces[PAIRED].start()
        for slot in (2, 6):
            pieces[slot].start()
            heads_even[slot].start()
        for slot in (4, 5, 1):
            pieces[slot].start()
        for slot in (4, 3, 7, 8):
            heads_even[slot].start()

    @pl.when((core == 0) & behind)
    def _():
        far_even()
        near_even()

    @pl.when((core == 0) & ahead)
    def _():
        near_even()
        pl.semaphore_wait(far_sem, 3)
        tell(ready_sem, sibling)
        far_even()

    @pl.when(core == 1)
    def _():
        pieces[PAIRED].start()
        for slot in (2, 6, 4, 5, 1):
            pieces[slot].start()
            heads_odd[slot].start()
        pl.semaphore_wait(ready_sem, 1)
        for slot in (3, 7, 8):
            pieces[slot].start()
        for slot in (3, 7, 8):
            heads_odd[slot].start()

    tail_ref[...] = jnp.zeros(tail_ref.shape, jnp.float32)
    tail_ref[:, : width - 1] = short_ref[...]
    best_ref[...] = jnp.full(best_ref.shape, LOW, jnp.float32)

    @pl.when(behind)
    def _():
        fill_bounds()

    def base_of(slot, row):
        d_blk, d_plane = PLACE[slot]
        g = at_plane(d_plane) * 2 + core
        mine = plane * 2 + row
        if d_blk == 0:
            step = g - mine
            return jnp.where(step == 0, base_own, far - unit * step)
        if d_blk == 1:
            return far - unit * jnp.where(blk == blocks - 1, 17, groups + g - mine)
        return far + unit * jnp.where(blk == 0, 17, groups + mine - g)

    def is_last(d_blk, d_plane, c):
        return (blk + d_blk == blocks - 1) & (at_plane(d_plane) == planes - 1) & (c == 1)

    def windows(slot, over):
        line = x_ref[slot]
        rest = jnp.where(over, tail_ref[...], line[:, count:])
        return normal_windows(jnp.concatenate([line[:, :count], rest], 1), count, width)

    def pieces_in(slot):
        return pltpu.make_async_remote_copy(
            src_ref=own_ref, dst_ref=x_ref.at[slot, :, :count], send_sem=send_sem.at[0],
            recv_sem=recv_sem.at[slot], device_id=sibling, device_id_type=MESH,
        )

    def head_in(slot):
        return pltpu.make_async_remote_copy(
            src_ref=own_ref.at[:, :LANES], dst_ref=x_ref.at[slot, :, count:], send_sem=send_sem.at[0],
            recv_sem=head_sem.at[slot], device_id=sibling, device_id_type=MESH,
        )

    relays = [
        pltpu.make_async_remote_copy(
            src_ref=x_ref.at[0, :, count:], dst_ref=x_ref.at[slot, :, count:], send_sem=send_sem.at[20 + at],
            recv_sem=head_sem.at[slot], device_id=device(-at, -1, 1), device_id_type=MESH,
        )
        for at, slot in enumerate((1, 5))
    ]

    pieces_in(PAIRED).wait_recv()

    @pl.when(core == 0)
    def _():
        x_ref[0, :, count:] = x_ref[PAIRED, :, :LANES]
        pltpu.make_async_remote_copy(
            src_ref=own_ref.at[:, :LANES], dst_ref=x_ref.at[PAIRED, :, count:], send_sem=send_sem.at[0],
            recv_sem=head_sem.at[0], device_id=sibling, device_id_type=MESH,
        ).wait_recv()

    @pl.when(core == 1)
    def _():
        x_ref[PAIRED, :, count:] = own_ref[:, :LANES]
        head_in(0).wait_recv()
        for copy in relays:
            copy.start()

    for row in range(2):
        slot = jnp.where(core == row, 0, PAIRED)
        put_rows(rows_ref.at[pl.ds(row * count, count)], windows(slot, is_last(0, 0, row)))

    slots = len(PLACE)
    last_plane = plane == planes - 1
    shared = (jnp.where(last_plane, 1, 2), jnp.where(last_plane, 2, 1))
    common = (4, 0, 3, 7, 8)
    order = [
        jnp.where(first_plane, at_first, jnp.where(last_plane, at_last, between))
        for at_first, at_last, between in zip((6, 4, 0, 5) + common[2:], (5, 6) + common, (6, 5) + common)
    ]
    opens = blk == 0
    closes = blk == blocks - 1
    order[6] = jnp.where(opens, 0, 8)
    last_list = [is_last(*PLACE[slot], core) for slot in range(slots)]
    base_lists = [[base_of(slot, row) for slot in range(slots)] for row in range(2)]
    step_list = [PLACE[slot][0] for slot in range(slots)]
    plane_list = [PLACE[slot][1] for slot in range(slots)]
    back_list = [-1, 4, 3, -1, 0, 2, 1, -1, -1]

    def build(slot, ref):
        put_columns(ref, windows(slot, pick(slot, last_list)))

    def arrive(slot):
        @pl.when(slot != 0)
        def _():
            pieces_in(slot).wait_recv()
            head_in(slot).wait_recv()

    def back(slot, at, target):
        return pltpu.make_async_remote_copy(
            src_ref=cols_ref.at[slot], dst_ref=got_ref.at[at], send_sem=back_send_sem.at[slot],
            recv_sem=back_recv_sem.at[at], device_id=target, device_id_type=MESH,
        )

    def give_back(slot):
        back(slot, pick(slot, back_list), device(pick(slot, step_list), pick(slot, plane_list), core)).start()

    def meet_shared(slot, now_ref):
        one = jnp.where(slot == 2, 1 - core, core)
        whole = plane == jnp.where(slot == 2, 1, planes - 1)
        low = jnp.where(whole, 0, one)
        high = jnp.where(whole, 2, jnp.where(first_plane, one, one + 1))
        cols_ref[slot] = jnp.full((1, count), LOW, jnp.float32)

        def body(at, _):
            base = jnp.where(at == 0, pick(slot, base_lists[0]), pick(slot, base_lists[1]))
            top = tile(rows_ref, now_ref, best_ref, limit_ref, at, base)
            cols_ref[slot] = jnp.maximum(cols_ref[slot], top)
            return 0

        lax.fori_loop(low, high, body, 0)

        @pl.when(plane != 0)
        def _():
            give_back(slot)

    def meet(slot, now_ref):
        tops = [
            tile(rows_ref, now_ref, best_ref, limit_ref, row, pick(slot, base_lists[row]))
            for row in range(2)
        ]
        cols_ref[slot] = jnp.maximum(*tops)

        beyond = closes & (pick(slot, step_list) == 1)

        @pl.when((pick(slot, back_list) >= 0) & jnp.logical_not(beyond))
        def _():
            give_back(slot)

    @pl.when(plane != 0)
    def _():
        arrive(shared[0])
        build(shared[0], even_ref)

    meet_shared(shared[0], even_ref)
    arrive(order[0])
    build(order[0], odd_ref)

    @pl.when(plane != 0)
    def _():
        arrive(shared[1])
        build(shared[1], even_ref)

    meet_shared(shared[1], even_ref)

    def pair(i, _):
        k = 2 * i
        now, then, after = (pick(k + at, order) for at in range(3))
        arrive(then)
        build(then, even_ref)
        meet(now, odd_ref)
        arrive(after)
        build(after, odd_ref)
        meet(then, even_ref)
        return 0

    lax.fori_loop(0, 3, pair, 0)
    def meet_last(row):
        @pl.when(jnp.logical_not(opens))
        def _():
            base = jnp.where(row == 0, base_lists[0][8], base_lists[1][8])
            tile(rows_ref, odd_ref, best_ref, limit_ref, row, base)

    @pl.when(opens)
    def _():
        arrive(8)

    meet_last(1 - core)

    @pl.when(plane == 0)
    def _():
        for slot in (1, 2):
            arrive(slot)

    def row_tops(row):
        return jnp.max(jnp.transpose(best_ref[pl.ds(row * count, count), :]), 0, keepdims=True)

    cols_ref[9] = row_tops(1 - core)
    back(9, 5, sibling).start()
    meet_last(core)
    top = jnp.maximum(row_tops(core), cols_ref[0])
    for slot in range(1, 10):
        pieces[slot].wait_send()

    @pl.when(core == 0)
    def _():
        for copy in heads_even.values():
            copy.wait_send()

    @pl.when(core == 1)
    def _():
        for copy in list(heads_odd.values()) + relays:
            copy.wait_send()

    back(9, 0, sibling).wait_send()

    @pl.when(jnp.logical_not(closes))
    def _():
        for slot in (4, 5, 6):
            back(slot, 0, sibling).wait_send()

    @pl.when(plane != 0)
    def _():
        for slot in (1, 2):
            back(slot, 0, sibling).wait_send()

    for slot, silent in ((3, planes - 1), (4, 1)):

        @pl.when(plane == silent)
        def _():
            got_ref[slot] = jnp.full((1, count), LOW, jnp.float32)

        @pl.when(plane != silent)
        def _():
            back(0, slot, sibling).wait_recv()

    back(0, 5, sibling).wait_recv()

    @pl.when(opens)
    def _():
        for slot in range(3):
            got_ref[slot] = jnp.full((1, count), LOW, jnp.float32)

    @pl.when(jnp.logical_not(opens))
    def _():
        for slot in range(3):
            back(0, slot, sibling).wait_recv()

    for slot in range(6):
        top = jnp.maximum(top, got_ref[slot])
    out_ref[...] = 1.0 - top * (1.0 / width)


def on_device(blocks, groups, series, tail, excl, band):
    count = series.shape[0]
    width = tail.shape[0] + 1
    hbm = pl.BlockSpec(memory_space=pltpu.HBM)
    window_cols = pltpu.VMEM((4 * width, count), jnp.bfloat16)
    out = pl.pallas_call(
        functools.partial(kernel, blocks, groups, width),
        out_shape=jax.ShapeDtypeStruct((1, count), jnp.float32),
        in_specs=[hbm, hbm, hbm, hbm],
        out_specs=pl.BlockSpec(memory_space=pltpu.VMEM),
        scratch_shapes=[
            pltpu.VMEM((1, count), jnp.float32),
            pltpu.VMEM((1, width - 1), jnp.float32),
            pltpu.VMEM((1, LANES), jnp.float32),
            pltpu.SMEM((1,), jnp.int32),
            pltpu.SMEM((1,), jnp.int32),
            pltpu.VMEM((10, 1, count + LANES), jnp.float32),
            pltpu.VMEM((2 * count, 4 * width), jnp.bfloat16),
            window_cols,
            window_cols,
            pltpu.VMEM((2 * count, LANES), jnp.float32),
            pltpu.VMEM((38 * count // SUBS, SUBS, LANES), jnp.float32),
            pltpu.VMEM((10, 1, count), jnp.float32),
            pltpu.VMEM((6, 1, count), jnp.float32),
            pltpu.SemaphoreType.DMA((4,)),
            pltpu.SemaphoreType.DMA((22,)),
            pltpu.SemaphoreType.DMA((10,)),
            pltpu.SemaphoreType.DMA((10,)),
            pltpu.SemaphoreType.DMA((10,)),
            pltpu.SemaphoreType.DMA((6,)),
            pltpu.SemaphoreType.REGULAR,
            pltpu.SemaphoreType.REGULAR,
        ],
        compiler_params=pltpu.CompilerParams(
            collective_id=0, has_side_effects=True, vmem_limit_bytes=48 * 1024 * 1024
        ),
    )(series.reshape(1, count), pltpu.with_memory_space_constraint(tail.reshape(1, width - 1), pltpu.HBM), excl, band)
    return out.reshape(count)


def solution(mesh):
    placed = (P(("blk", "merge")), P(), P(), P())
    body = functools.partial(on_device, mesh.shape["blk"], mesh.shape["merge"])
    return jax.shard_map(
        body, mesh=mesh, in_specs=placed, out_specs=P(("blk", "merge")), check_vma=False
    )
```

```python
import functools

import jax
import jax.numpy as jnp
from jax import lax
from jax.experimental import pallas as pl
from jax.experimental.pallas import tpu as pltpu
from jax.sharding import PartitionSpec as P

LOW = -192.0
LANES = 128
SUBS = 8
MESH = pl.DeviceIdType.MESH


def normal_windows(line, count, width):
    length = line.shape[1]
    rows = jnp.broadcast_to(line, (SUBS, length))
    parts = [
        pltpu.roll(rows, length - (width - 1) + first, 1, stride=1, stride_axis=0)[:, :count]
        for first in range(0, width, SUBS)
    ]
    mean = jnp.sum(functools.reduce(jnp.add, parts), 0, keepdims=True) * (1.0 / width)
    cent = [part - mean for part in parts]
    squares = functools.reduce(jnp.add, [part * part for part in cent])
    var = jnp.sum(squares, 0, keepdims=True) * (1.0 / width)
    inv = lax.rsqrt(var + 1e-06)
    return jnp.concatenate([part * inv for part in cent], 0)


def halves(z):
    high = z.astype(jnp.bfloat16)
    low = (z - high.astype(jnp.float32)).astype(jnp.bfloat16)
    return high, low


def put_columns(ref, z):
    high, low = halves(z)
    width = z.shape[0]
    for at, part in enumerate((high, low, high, low)):
        ref[at * width : (at + 1) * width, :] = part


def put_rows(ref, z):
    high, low = halves(jnp.transpose(z))
    width = z.shape[0]
    ref[:, : 2 * width] = jnp.concatenate([high, high], 1)
    ref[:, 2 * width :] = jnp.concatenate([low, low], 1)


def tile(rows_ref, cols_ref, best_ref, limit_ref, row, base):
    count = cols_ref.shape[1]
    mine = pl.ds(row * count, count)
    step = min(256, count)
    tops = []
    for first in range(0, count, step):
        corr = jnp.dot(
            rows_ref[mine, :], cols_ref[:, first : first + step], preferred_element_type=jnp.float32
        )
        best = None
        for lane in range(first, first + step, LANES):
            part = corr[:, lane - first : lane - first + LANES].reshape(count // SUBS, SUBS, LANES)
            limit = limit_ref[pl.ds(base - lane // SUBS, count // SUBS)]
            part = jnp.minimum(part, limit)
            tops.append(jnp.max(part, 0))
            best = part if best is None else jnp.maximum(best, part)
        best_ref[mine, :] = jnp.maximum(best_ref[mine, :], best.reshape(count, LANES))
    return jnp.max(jnp.concatenate(tops, 1), 0, keepdims=True)


def pick(k, entries):
    out = entries[-1]
    for at in range(len(entries) - 2, -1, -1):
        out = jnp.where(k == at, entries[at], out)
    return out


SPREAD = ((0, 1, 2), (0, -1, 1), (0, 2, 3), (-1, 0, 4), (-1, -1, 5), (-1, 1, 6), (-1, 2, 7), (1, 2, 8))
PLACE = ((0, 0), (0, 1), (0, -1), (0, 2), (1, 0), (1, 1), (1, -1), (1, 2), (-1, 2))
PAIRED = 9


def kernel(
    blocks, groups, width,
    series_hbm, tail_hbm, excl_hbm, band_hbm, out_ref,
    own_ref, short_ref, tail_ref, excl_ref, band_ref, x_ref, rows_ref, even_ref, odd_ref, best_ref, limit_ref,
    cols_ref, got_ref, local_sem, send_sem, recv_sem, head_sem, back_send_sem, back_recv_sem, ready_sem, far_sem,
):
    count = own_ref.shape[1]
    unit = count // SUBS
    planes = groups // 2
    blk = lax.axis_index("blk")
    grp = lax.axis_index("merge")
    plane = lax.div(grp, 2)
    core = lax.rem(grp, 2)

    def at_plane(d_plane):
        return lax.rem(plane + d_plane + 2 * planes, planes)

    def device(d_blk, d_plane, c):
        return (lax.rem(blk + d_blk + 2 * blocks, blocks), at_plane(d_plane) * 2 + c)

    sibling = device(0, 0, 1 - core)
    loads = [
        pltpu.make_async_copy(series_hbm, own_ref, local_sem.at[0]),
        pltpu.make_async_copy(tail_hbm, short_ref, local_sem.at[1]),
        pltpu.make_async_copy(excl_hbm, excl_ref, local_sem.at[2]),
        pltpu.make_async_copy(band_hbm, band_ref, local_sem.at[3]),
    ]
    for load in loads:
        load.start()

    barrier = pltpu.get_barrier_semaphore()

    def greet(target):
        pl.semaphore_signal(barrier, inc=1, device_id=target, device_id_type=MESH)

    ahead = plane < 2

    @pl.when(ahead)
    def _():
        for d_blk in (0, 1, -1):
            greet(device(d_blk, 2, 0))

    greet(sibling)
    for d_blk, d_plane in ((0, 1), (0, -1), (1, 0), (1, 1), (1, -1)):
        greet(device(d_blk, d_plane, 1))

    @pl.when(core == 1)
    def _():
        @pl.when(plane != 2)
        def _():
            greet((lax.rem(blk + 2, blocks), 1))

        @pl.when(plane != 1)
        def _():
            greet(device(-1, -1, 1))

    far = 18 * unit
    base_own = 37 * unit
    total = 38 * unit

    def fill_bounds():
        excl = excl_ref[0]
        band = band_ref[0]
        skew = lax.broadcasted_iota(jnp.int32, (16, SUBS, LANES), 2)
        skew = skew - lax.broadcasted_iota(jnp.int32, (16, SUBS, LANES), 1)
        skew = skew - SUBS * lax.broadcasted_iota(jnp.int32, (16, SUBS, LANES), 0)

        def fill(start, stop, diff_of, keep):
            def body(i, _):
                at = start + i * 16
                limit_ref[pl.ds(at, 16)] = jnp.where(keep(diff_of(at)), -LOW, LOW)
                return 0

            lax.fori_loop(0, (stop - start) // 16, body, 0)

        inside = lambda d: (d > excl) & (d <= band)
        fill(0, far, lambda at: skew + SUBS * (far - at), inside)
        fill(far, 2 * far, lambda at: SUBS * (at - far) - skew, inside)
        fill(2 * far, total, lambda at: skew + SUBS * (base_own - at), lambda d: jnp.abs(d) > excl)

    for load in loads:
        load.wait()
    x_ref[0, :, :count] = own_ref[...]

    @pl.when(ahead)
    def _():
        fill_bounds()

    first_plane = plane == 0
    far_count = jnp.where(ahead, 1, 7)
    near_count = 11 + jnp.where(first_plane, 3, 1)
    pl.semaphore_wait(barrier, jnp.where(core == 0, far_count, near_count))

    def tell(sem, target):
        pl.semaphore_signal(sem, inc=1, device_id=target, device_id_type=MESH)

    behind = jnp.logical_not(ahead)

    @pl.when((core == 1) | behind)
    def _():
        tell(ready_sem, sibling)

    @pl.when((core == 0) & behind)
    def _():
        for d_blk in (0, 1, -1):
            tell(far_sem, device(d_blk, 2, 0))


    def send_piece(slot, target):
        return pltpu.make_async_remote_copy(
            src_ref=own_ref, dst_ref=x_ref.at[slot, :, :count], send_sem=send_sem.at[slot],
            recv_sem=recv_sem.at[slot], device_id=target, device_id_type=MESH,
        )

    def send_head(slot, at, target):
        return pltpu.make_async_remote_copy(
            src_ref=own_ref.at[:, :LANES], dst_ref=x_ref.at[slot, :, count:], send_sem=send_sem.at[10 + at],
            recv_sem=head_sem.at[0 if at in (0, 9) else at], device_id=target, device_id_type=MESH,
        )

    back_blk = jnp.where(first_plane, -1, 0)
    pieces = {slot: send_piece(slot, device(d, dp, core)) for d, dp, slot in SPREAD}
    pieces[PAIRED] = send_piece(PAIRED, sibling)
    heads_odd = {slot: send_head(slot, slot, device(d, dp, 0)) for d, dp, slot in SPREAD}
    heads_even = {
        slot: send_head(slot, slot, device(back_blk + d, dp - 1, 1)) for d, dp, slot in SPREAD if dp != -1
    }
    heads_even[0] = send_head(0, 0, device(back_blk, -1, 1))
    heads_even[9] = send_head(PAIRED, 9, device(back_blk, -1, 0))

    def far_even():
        for slot in (3, 7, 8):
            pieces[slot].start()

    def near_even():
        pl.semaphore_wait(ready_sem, 1)
        for slot in (0, 9):
            heads_even[slot].start()
        pieces[PAIRED].start()
        for slot in (2, 6):
            pieces[slot].start()
            heads_even[slot].start()
        for slot in (4, 5, 1):
            pieces[slot].start()
        for slot in (4, 3, 7, 8):
            heads_even[slot].start()

    @pl.when((core == 0) & behind)
    def _():
        far_even()
        near_even()

    @pl.when((core == 0) & ahead)
    def _():
        near_even()
        pl.semaphore_wait(far_sem, 3)
        tell(ready_sem, sibling)
        far_even()

    @pl.when(core == 1)
    def _():
        pieces[PAIRED].start()
        for slot in (2, 6, 4, 5, 1):
            pieces[slot].start()
            heads_odd[slot].start()
        pl.semaphore_wait(ready_sem, 1)
        for slot in (3, 7, 8):
            pieces[slot].start()
        for slot in (3, 7, 8):
            heads_odd[slot].start()

    tail_ref[...] = jnp.zeros(tail_ref.shape, jnp.float32)
    tail_ref[:, : width - 1] = short_ref[...]
    best_ref[...] = jnp.full(best_ref.shape, LOW, jnp.float32)

    @pl.when(behind)
    def _():
        fill_bounds()

    def base_of(slot, row):
        d_blk, d_plane = PLACE[slot]
        g = at_plane(d_plane) * 2 + core
        mine = plane * 2 + row
        if d_blk == 0:
            step = g - mine
            return jnp.where(step == 0, base_own, far - unit * step)
        if d_blk == 1:
            return far - unit * jnp.where(blk == blocks - 1, 17, groups + g - mine)
        return far + unit * jnp.where(blk == 0, 17, groups + mine - g)

    def is_last(d_blk, d_plane, c):
        return (blk + d_blk == blocks - 1) & (at_plane(d_plane) == planes - 1) & (c == 1)

    def windows(slot, over):
        line = x_ref[slot]
        rest = jnp.where(over, tail_ref[...], line[:, count:])
        return normal_windows(jnp.concatenate([line[:, :count], rest], 1), count, width)

    def pieces_in(slot):
        return pltpu.make_async_remote_copy(
            src_ref=own_ref, dst_ref=x_ref.at[slot, :, :count], send_sem=send_sem.at[0],
            recv_sem=recv_sem.at[slot], device_id=sibling, device_id_type=MESH,
        )

    def head_in(slot):
        return pltpu.make_async_remote_copy(
            src_ref=own_ref.at[:, :LANES], dst_ref=x_ref.at[slot, :, count:], send_sem=send_sem.at[0],
            recv_sem=head_sem.at[slot], device_id=sibling, device_id_type=MESH,
        )

    relays = [
        pltpu.make_async_remote_copy(
            src_ref=x_ref.at[0, :, count:], dst_ref=x_ref.at[slot, :, count:], send_sem=send_sem.at[20 + at],
            recv_sem=head_sem.at[slot], device_id=device(-at, -1, 1), device_id_type=MESH,
        )
        for at, slot in enumerate((1, 5))
    ]

    pieces_in(PAIRED).wait_recv()

    @pl.when(core == 0)
    def _():
        x_ref[0, :, count:] = x_ref[PAIRED, :, :LANES]
        pltpu.make_async_remote_copy(
            src_ref=own_ref.at[:, :LANES], dst_ref=x_ref.at[PAIRED, :, count:], send_sem=send_sem.at[0],
            recv_sem=head_sem.at[0], device_id=sibling, device_id_type=MESH,
        ).wait_recv()

    @pl.when(core == 1)
    def _():
        x_ref[PAIRED, :, count:] = own_ref[:, :LANES]
        head_in(0).wait_recv()
        for copy in relays:
            copy.start()

    for row in range(2):
        slot = jnp.where(core == row, 0, PAIRED)
        put_rows(rows_ref.at[pl.ds(row * count, count)], windows(slot, is_last(0, 0, row)))

    slots = len(PLACE)
    last_plane = plane == planes - 1
    shared = (jnp.where(last_plane, 1, 2), jnp.where(last_plane, 2, 1))
    common = (4, 0, 3, 7, 8)
    order = [
        jnp.where(first_plane, at_first, jnp.where(last_plane, at_last, between))
        for at_first, at_last, between in zip((6, 4, 0, 5) + common[2:], (5, 6) + common, (6, 5) + common)
    ]
    opens = blk == 0
    closes = blk == blocks - 1
    order[6] = jnp.where(opens, 0, 8)
    last_list = [is_last(*PLACE[slot], core) for slot in range(slots)]
    base_lists = [[base_of(slot, row) for slot in range(slots)] for row in range(2)]
    step_list = [PLACE[slot][0] for slot in range(slots)]
    plane_list = [PLACE[slot][1] for slot in range(slots)]
    back_list = [-1, 4, 3, -1, 0, 2, 1, -1, -1]

    def build(slot, ref):
        put_columns(ref, windows(slot, pick(slot, last_list)))

    def arrive(slot):
        @pl.when(slot != 0)
        def _():
            pieces_in(slot).wait_recv()
            head_in(slot).wait_recv()

    def back(slot, at, target):
        return pltpu.make_async_remote_copy(
            src_ref=cols_ref.at[slot], dst_ref=got_ref.at[at], send_sem=back_send_sem.at[slot],
            recv_sem=back_recv_sem.at[at], device_id=target, device_id_type=MESH,
        )

    def give_back(slot):
        back(slot, pick(slot, back_list), device(pick(slot, step_list), pick(slot, plane_list), core)).start()

    def meet_shared(slot, now_ref):
        one = jnp.where(slot == 2, 1 - core, core)
        whole = plane == jnp.where(slot == 2, 1, planes - 1)
        low = jnp.where(whole, 0, one)
        high = jnp.where(whole, 2, jnp.where(first_plane, one, one + 1))
        cols_ref[slot] = jnp.full((1, count), LOW, jnp.float32)

        def body(at, _):
            base = jnp.where(at == 0, pick(slot, base_lists[0]), pick(slot, base_lists[1]))
            top = tile(rows_ref, now_ref, best_ref, limit_ref, at, base)
            cols_ref[slot] = jnp.maximum(cols_ref[slot], top)
            return 0

        lax.fori_loop(low, high, body, 0)

        @pl.when(plane != 0)
        def _():
            give_back(slot)

    def meet(slot, now_ref):
        tops = [
            tile(rows_ref, now_ref, best_ref, limit_ref, row, pick(slot, base_lists[row]))
            for row in range(2)
        ]
        cols_ref[slot] = jnp.maximum(*tops)

        beyond = closes & (pick(slot, step_list) == 1)

        @pl.when((pick(slot, back_list) >= 0) & jnp.logical_not(beyond))
        def _():
            give_back(slot)

    arrive(order[0])
    build(order[0], odd_ref)

    @pl.when(plane != 0)
    def _():
        arrive(shared[0])
        build(shared[0], even_ref)

    meet(order[0], odd_ref)
    arrive(order[1])
    build(order[1], odd_ref)
    meet_shared(shared[0], even_ref)

    @pl.when(plane != 0)
    def _():
        arrive(shared[1])
        build(shared[1], even_ref)

    meet_shared(shared[1], even_ref)

    def pair(i, _):
        k = 2 * i + 1
        now, then, after = (pick(k + at, order) for at in range(3))
        arrive(then)
        build(then, even_ref)
        meet(now, odd_ref)
        arrive(after)
        build(after, odd_ref)
        meet(then, even_ref)
        return 0

    lax.fori_loop(0, 2, pair, 0)
    arrive(order[6])
    build(order[6], even_ref)
    meet(order[5], odd_ref)

    def meet_last(row):
        @pl.when(jnp.logical_not(opens))
        def _():
            base = jnp.where(row == 0, base_lists[0][8], base_lists[1][8])
            tile(rows_ref, even_ref, best_ref, limit_ref, row, base)

    @pl.when(opens)
    def _():
        arrive(8)

    meet_last(1 - core)

    @pl.when(plane == 0)
    def _():
        for slot in (1, 2):
            arrive(slot)

    def row_tops(row):
        return jnp.max(jnp.transpose(best_ref[pl.ds(row * count, count), :]), 0, keepdims=True)

    cols_ref[9] = row_tops(1 - core)
    back(9, 5, sibling).start()
    meet_last(core)
    top = jnp.maximum(row_tops(core), cols_ref[0])
    for slot in range(1, 10):
        pieces[slot].wait_send()

    @pl.when(core == 0)
    def _():
        for copy in heads_even.values():
            copy.wait_send()

    @pl.when(core == 1)
    def _():
        for copy in list(heads_odd.values()) + relays:
            copy.wait_send()

    back(9, 0, sibling).wait_send()

    @pl.when(jnp.logical_not(closes))
    def _():
        for slot in (4, 5, 6):
            back(slot, 0, sibling).wait_send()

    @pl.when(plane != 0)
    def _():
        for slot in (1, 2):
            back(slot, 0, sibling).wait_send()

    for slot, silent in ((3, planes - 1), (4, 1)):

        @pl.when(plane == silent)
        def _():
            got_ref[slot] = jnp.full((1, count), LOW, jnp.float32)

        @pl.when(plane != silent)
        def _():
            back(0, slot, sibling).wait_recv()

    back(0, 5, sibling).wait_recv()

    @pl.when(opens)
    def _():
        for slot in range(3):
            got_ref[slot] = jnp.full((1, count), LOW, jnp.float32)

    @pl.when(jnp.logical_not(opens))
    def _():
        for slot in range(3):
            back(0, slot, sibling).wait_recv()

    for slot in range(6):
        top = jnp.maximum(top, got_ref[slot])
    out_ref[...] = 1.0 - top * (1.0 / width)


def on_device(blocks, groups, series, tail, excl, band):
    count = series.shape[0]
    width = tail.shape[0] + 1
    hbm = pl.BlockSpec(memory_space=pltpu.HBM)
    window_cols = pltpu.VMEM((4 * width, count), jnp.bfloat16)
    out = pl.pallas_call(
        functools.partial(kernel, blocks, groups, width),
        out_shape=jax.ShapeDtypeStruct((1, count), jnp.float32),
        in_specs=[hbm, hbm, hbm, hbm],
        out_specs=pl.BlockSpec(memory_space=pltpu.VMEM),
        scratch_shapes=[
            pltpu.VMEM((1, count), jnp.float32),
            pltpu.VMEM((1, width - 1), jnp.float32),
            pltpu.VMEM((1, LANES), jnp.float32),
            pltpu.SMEM((1,), jnp.int32),
            pltpu.SMEM((1,), jnp.int32),
            pltpu.VMEM((10, 1, count + LANES), jnp.float32),
            pltpu.VMEM((2 * count, 4 * width), jnp.bfloat16),
            window_cols,
            window_cols,
            pltpu.VMEM((2 * count, LANES), jnp.float32),
            pltpu.VMEM((38 * count // SUBS, SUBS, LANES), jnp.float32),
            pltpu.VMEM((10, 1, count), jnp.float32),
            pltpu.VMEM((6, 1, count), jnp.float32),
            pltpu.SemaphoreType.DMA((4,)),
            pltpu.SemaphoreType.DMA((22,)),
            pltpu.SemaphoreType.DMA((10,)),
            pltpu.SemaphoreType.DMA((10,)),
            pltpu.SemaphoreType.DMA((10,)),
            pltpu.SemaphoreType.DMA((6,)),
            pltpu.SemaphoreType.REGULAR,
            pltpu.SemaphoreType.REGULAR,
        ],
        compiler_params=pltpu.CompilerParams(
            collective_id=0, has_side_effects=True, vmem_limit_bytes=48 * 1024 * 1024
        ),
    )(series.reshape(1, count), pltpu.with_memory_space_constraint(tail.reshape(1, width - 1), pltpu.HBM), excl, band)
    return out.reshape(count)


def solution(mesh):
    placed = (P(("blk", "merge")), P(), P(), P())
    body = functools.partial(on_device, mesh.shape["blk"], mesh.shape["merge"])
    return jax.shard_map(
        body, mesh=mesh, in_specs=placed, out_specs=P(("blk", "merge")), check_vma=False
    )
```

```python
import functools

import jax
import jax.numpy as jnp
from jax import lax
from jax.experimental import pallas as pl
from jax.experimental.pallas import tpu as pltpu
from jax.sharding import PartitionSpec as P

LOW = -192.0
LANES = 128
SUBS = 8
MESH = pl.DeviceIdType.MESH


def normal_windows(line, count, width):
    length = line.shape[1]
    rows = jnp.broadcast_to(line, (SUBS, length))
    parts = [
        pltpu.roll(rows, length - (width - 1) + first, 1, stride=1, stride_axis=0)[:, :count]
        for first in range(0, width, SUBS)
    ]
    mean = jnp.sum(functools.reduce(jnp.add, parts), 0, keepdims=True) * (1.0 / width)
    cent = [part - mean for part in parts]
    squares = functools.reduce(jnp.add, [part * part for part in cent])
    var = jnp.sum(squares, 0, keepdims=True) * (1.0 / width)
    inv = lax.rsqrt(var + 1e-06)
    return jnp.concatenate([part * inv for part in cent], 0)


def halves(z):
    high = z.astype(jnp.bfloat16)
    low = (z - high.astype(jnp.float32)).astype(jnp.bfloat16)
    return high, low


def put_columns(ref, z):
    high, low = halves(z)
    width = z.shape[0]
    for at, part in enumerate((high, low, high, low)):
        ref[at * width : (at + 1) * width, :] = part


def put_rows(ref, z):
    high, low = halves(jnp.transpose(z))
    width = z.shape[0]
    ref[:, : 2 * width] = jnp.concatenate([high, high], 1)
    ref[:, 2 * width :] = jnp.concatenate([low, low], 1)


def tile(rows_ref, cols_ref, best_ref, limit_ref, row, base):
    count = cols_ref.shape[1]
    mine = pl.ds(row * count, count)
    step = min(256, count)
    tops = []
    for first in range(0, count, step):
        corr = jnp.dot(
            rows_ref[mine, :], cols_ref[:, first : first + step], preferred_element_type=jnp.float32
        )
        best = None
        for lane in range(first, first + step, LANES):
            part = corr[:, lane - first : lane - first + LANES].reshape(count // SUBS, SUBS, LANES)
            limit = limit_ref[pl.ds(base - lane // SUBS, count // SUBS)]
            part = jnp.minimum(part, limit)
            tops.append(jnp.max(part, 0))
            best = part if best is None else jnp.maximum(best, part)
        best_ref[mine, :] = jnp.maximum(best_ref[mine, :], best.reshape(count, LANES))
    return jnp.max(jnp.concatenate(tops, 1), 0, keepdims=True)


def pick(k, entries):
    out = entries[-1]
    for at in range(len(entries) - 2, -1, -1):
        out = jnp.where(k == at, entries[at], out)
    return out


SPREAD = ((0, 1, 2), (0, -1, 1), (0, 2, 3), (-1, 0, 4), (-1, -1, 5), (-1, 1, 6), (-1, 2, 7), (1, 2, 8))
PLACE = ((0, 0), (0, 1), (0, -1), (0, 2), (1, 0), (1, 1), (1, -1), (1, 2), (-1, 2))
PAIRED = 9


def kernel(
    blocks, groups, width,
    series_hbm, tail_hbm, excl_hbm, band_hbm, out_ref,
    own_ref, short_ref, tail_ref, excl_ref, band_ref, x_ref, rows_ref, even_ref, odd_ref, best_ref, limit_ref,
    cols_ref, got_ref, local_sem, send_sem, recv_sem, head_sem, back_send_sem, back_recv_sem, ready_sem, far_sem,
):
    count = own_ref.shape[1]
    unit = count // SUBS
    planes = groups // 2
    blk = lax.axis_index("blk")
    grp = lax.axis_index("merge")
    plane = lax.div(grp, 2)
    core = lax.rem(grp, 2)

    def at_plane(d_plane):
        return lax.rem(plane + d_plane + 2 * planes, planes)

    def device(d_blk, d_plane, c):
        return (lax.rem(blk + d_blk + 2 * blocks, blocks), at_plane(d_plane) * 2 + c)

    sibling = device(0, 0, 1 - core)
    loads = [
        pltpu.make_async_copy(series_hbm, own_ref, local_sem.at[0]),
        pltpu.make_async_copy(tail_hbm, short_ref, local_sem.at[1]),
        pltpu.make_async_copy(excl_hbm, excl_ref, local_sem.at[2]),
        pltpu.make_async_copy(band_hbm, band_ref, local_sem.at[3]),
    ]
    for load in loads:
        load.start()

    barrier = pltpu.get_barrier_semaphore()

    def greet(target):
        pl.semaphore_signal(barrier, inc=1, device_id=target, device_id_type=MESH)

    ahead = plane < 2

    @pl.when(ahead)
    def _():
        for d_blk in (0, 1, -1):
            greet(device(d_blk, 2, 0))

    greet(sibling)
    for d_blk, d_plane in ((0, 1), (0, -1), (1, 0), (1, 1), (1, -1)):
        greet(device(d_blk, d_plane, 1))

    @pl.when(core == 1)
    def _():
        @pl.when(plane != 2)
        def _():
            greet((lax.rem(blk + 2, blocks), 1))

        @pl.when(plane != 1)
        def _():
            greet(device(-1, -1, 1))

    far = 18 * unit
    base_own = 37 * unit
    total = 38 * unit

    def fill_bounds():
        excl = excl_ref[0]
        band = band_ref[0]
        skew = lax.broadcasted_iota(jnp.int32, (16, SUBS, LANES), 2)
        skew = skew - lax.broadcasted_iota(jnp.int32, (16, SUBS, LANES), 1)
        skew = skew - SUBS * lax.broadcasted_iota(jnp.int32, (16, SUBS, LANES), 0)

        def fill(start, stop, diff_of, keep):
            def body(i, _):
                at = start + i * 16
                limit_ref[pl.ds(at, 16)] = jnp.where(keep(diff_of(at)), -LOW, LOW)
                return 0

            lax.fori_loop(0, (stop - start) // 16, body, 0)

        inside = lambda d: (d > excl) & (d <= band)
        fill(0, far, lambda at: skew + SUBS * (far - at), inside)
        fill(far, 2 * far, lambda at: SUBS * (at - far) - skew, inside)
        fill(2 * far, total, lambda at: skew + SUBS * (base_own - at), lambda d: jnp.abs(d) > excl)

    for load in loads:
        load.wait()
    x_ref[0, :, :count] = own_ref[...]

    @pl.when(ahead)
    def _():
        fill_bounds()

    first_plane = plane == 0
    far_count = jnp.where(ahead, 1, 7)
    near_count = 11 + jnp.where(first_plane, 3, 1)
    pl.semaphore_wait(barrier, jnp.where(core == 0, far_count, near_count))

    def tell(sem, target):
        pl.semaphore_signal(sem, inc=1, device_id=target, device_id_type=MESH)

    behind = jnp.logical_not(ahead)

    @pl.when((core == 1) | behind)
    def _():
        tell(ready_sem, sibling)

    @pl.when((core == 0) & behind)
    def _():
        for d_blk in (0, 1, -1):
            tell(far_sem, device(d_blk, 2, 0))


    def send_piece(slot, target):
        return pltpu.make_async_remote_copy(
            src_ref=own_ref, dst_ref=x_ref.at[slot, :, :count], send_sem=send_sem.at[slot],
            recv_sem=recv_sem.at[slot], device_id=target, device_id_type=MESH,
        )

    def send_head(slot, at, target):
        return pltpu.make_async_remote_copy(
            src_ref=own_ref.at[:, :LANES], dst_ref=x_ref.at[slot, :, count:], send_sem=send_sem.at[10 + at],
            recv_sem=head_sem.at[0 if at in (0, 9) else at], device_id=target, device_id_type=MESH,
        )

    back_blk = jnp.where(first_plane, -1, 0)
    pieces = {slot: send_piece(slot, device(d, dp, core)) for d, dp, slot in SPREAD}
    pieces[PAIRED] = send_piece(PAIRED, sibling)
    heads_odd = {slot: send_head(slot, slot, device(d, dp, 0)) for d, dp, slot in SPREAD}
    heads_even = {
        slot: send_head(slot, slot, device(back_blk + d, dp - 1, 1)) for d, dp, slot in SPREAD if dp != -1
    }
    heads_even[0] = send_head(0, 0, device(back_blk, -1, 1))
    heads_even[9] = send_head(PAIRED, 9, device(back_blk, -1, 0))

    def far_even():
        for slot in (3, 7, 8):
            pieces[slot].start()

    def near_even():
        pl.semaphore_wait(ready_sem, 1)
        for slot in (0, 9):
            heads_even[slot].start()
        pieces[PAIRED].start()
        for slot in (2, 6):
            pieces[slot].start()
            heads_even[slot].start()
        for slot in (4, 5, 1):
            pieces[slot].start()
        for slot in (4, 3, 7, 8):
            heads_even[slot].start()

    @pl.when((core == 0) & behind)
    def _():
        far_even()
        near_even()

    @pl.when((core == 0) & ahead)
    def _():
        near_even()
        pl.semaphore_wait(far_sem, 3)
        tell(ready_sem, sibling)
        far_even()

    @pl.when(core == 1)
    def _():
        pieces[PAIRED].start()
        for slot in (2, 6, 4, 5, 1):
            pieces[slot].start()
            heads_odd[slot].start()
        pl.semaphore_wait(ready_sem, 1)
        for slot in (3, 7, 8):
            pieces[slot].start()
        for slot in (3, 7, 8):
            heads_odd[slot].start()

    tail_ref[...] = jnp.zeros(tail_ref.shape, jnp.float32)
    tail_ref[:, : width - 1] = short_ref[...]
    best_ref[...] = jnp.full(best_ref.shape, LOW, jnp.float32)

    @pl.when(behind)
    def _():
        fill_bounds()

    def base_of(slot, row):
        d_blk, d_plane = PLACE[slot]
        g = at_plane(d_plane) * 2 + core
        mine = plane * 2 + row
        if d_blk == 0:
            step = g - mine
            return jnp.where(step == 0, base_own, far - unit * step)
        if d_blk == 1:
            return far - unit * jnp.where(blk == blocks - 1, 17, groups + g - mine)
        return far + unit * jnp.where(blk == 0, 17, groups + mine - g)

    def is_last(d_blk, d_plane, c):
        return (blk + d_blk == blocks - 1) & (at_plane(d_plane) == planes - 1) & (c == 1)

    def windows(slot, over):
        line = x_ref[slot]
        rest = jnp.where(over, tail_ref[...], line[:, count:])
        return normal_windows(jnp.concatenate([line[:, :count], rest], 1), count, width)

    def pieces_in(slot):
        return pltpu.make_async_remote_copy(
            src_ref=own_ref, dst_ref=x_ref.at[slot, :, :count], send_sem=send_sem.at[0],
            recv_sem=recv_sem.at[slot], device_id=sibling, device_id_type=MESH,
        )

    def head_in(slot):
        return pltpu.make_async_remote_copy(
            src_ref=own_ref.at[:, :LANES], dst_ref=x_ref.at[slot, :, count:], send_sem=send_sem.at[0],
            recv_sem=head_sem.at[slot], device_id=sibling, device_id_type=MESH,
        )

    relays = [
        pltpu.make_async_remote_copy(
            src_ref=x_ref.at[0, :, count:], dst_ref=x_ref.at[slot, :, count:], send_sem=send_sem.at[20 + at],
            recv_sem=head_sem.at[slot], device_id=device(-at, -1, 1), device_id_type=MESH,
        )
        for at, slot in enumerate((1, 5))
    ]

    pieces_in(PAIRED).wait_recv()

    @pl.when(core == 0)
    def _():
        x_ref[0, :, count:] = x_ref[PAIRED, :, :LANES]
        pltpu.make_async_remote_copy(
            src_ref=own_ref.at[:, :LANES], dst_ref=x_ref.at[PAIRED, :, count:], send_sem=send_sem.at[0],
            recv_sem=head_sem.at[0], device_id=sibling, device_id_type=MESH,
        ).wait_recv()

    @pl.when(core == 1)
    def _():
        x_ref[PAIRED, :, count:] = own_ref[:, :LANES]
        head_in(0).wait_recv()
        for copy in relays:
            copy.start()

    for row in range(2):
        slot = jnp.where(core == row, 0, PAIRED)
        put_rows(rows_ref.at[pl.ds(row * count, count)], windows(slot, is_last(0, 0, row)))

    slots = len(PLACE)
    last_plane = plane == planes - 1
    shared = (jnp.where(last_plane, 1, 2), jnp.where(last_plane, 2, 1))
    common = (4, 0, 3, 7, 8)
    order = [
        jnp.where(first_plane, at_first, jnp.where(last_plane, at_last, between))
        for at_first, at_last, between in zip((4, 6, 0, 5) + common[2:], (5, 6) + common, (6, 5) + common)
    ]
    opens = blk == 0
    closes = blk == blocks - 1
    order[6] = jnp.where(opens, 0, 8)
    last_list = [is_last(*PLACE[slot], core) for slot in range(slots)]
    base_lists = [[base_of(slot, row) for slot in range(slots)] for row in range(2)]
    step_list = [PLACE[slot][0] for slot in range(slots)]
    plane_list = [PLACE[slot][1] for slot in range(slots)]
    back_list = [-1, 4, 3, -1, 0, 2, 1, -1, -1]

    def build(slot, ref):
        put_columns(ref, windows(slot, pick(slot, last_list)))

    def arrive(slot):
        @pl.when(slot != 0)
        def _():
            pieces_in(slot).wait_recv()
            head_in(slot).wait_recv()

    def back(slot, at, target):
        return pltpu.make_async_remote_copy(
            src_ref=cols_ref.at[slot], dst_ref=got_ref.at[at], send_sem=back_send_sem.at[slot],
            recv_sem=back_recv_sem.at[at], device_id=target, device_id_type=MESH,
        )

    def give_back(slot):
        back(slot, pick(slot, back_list), device(pick(slot, step_list), pick(slot, plane_list), core)).start()

    def meet_shared(slot, now_ref):
        one = jnp.where(slot == 2, 1 - core, core)
        whole = plane == jnp.where(slot == 2, 1, planes - 1)
        low = jnp.where(whole, 0, one)
        high = jnp.where(whole, 2, jnp.where(first_plane, one, one + 1))
        cols_ref[slot] = jnp.full((1, count), LOW, jnp.float32)

        def body(at, _):
            base = jnp.where(at == 0, pick(slot, base_lists[0]), pick(slot, base_lists[1]))
            top = tile(rows_ref, now_ref, best_ref, limit_ref, at, base)
            cols_ref[slot] = jnp.maximum(cols_ref[slot], top)
            return 0

        lax.fori_loop(low, high, body, 0)

        @pl.when(plane != 0)
        def _():
            give_back(slot)

    def meet(slot, now_ref):
        tops = [
            tile(rows_ref, now_ref, best_ref, limit_ref, row, pick(slot, base_lists[row]))
            for row in range(2)
        ]
        cols_ref[slot] = jnp.maximum(*tops)

        beyond = closes & (pick(slot, step_list) == 1)

        @pl.when((pick(slot, back_list) >= 0) & jnp.logical_not(beyond))
        def _():
            give_back(slot)

    arrive(order[0])
    build(order[0], odd_ref)

    @pl.when(plane != 0)
    def _():
        arrive(shared[0])
        build(shared[0], even_ref)

    meet(order[0], odd_ref)
    arrive(order[1])
    build(order[1], odd_ref)
    meet_shared(shared[0], even_ref)

    @pl.when(plane != 0)
    def _():
        arrive(shared[1])
        build(shared[1], even_ref)

    meet_shared(shared[1], even_ref)

    def pair(i, _):
        k = 2 * i + 1
        now, then, after = (pick(k + at, order) for at in range(3))
        arrive(then)
        build(then, even_ref)
        meet(now, odd_ref)
        arrive(after)
        build(after, odd_ref)
        meet(then, even_ref)
        return 0

    lax.fori_loop(0, 2, pair, 0)
    arrive(order[6])
    build(order[6], even_ref)
    meet(order[5], odd_ref)

    def meet_last(row):
        @pl.when(jnp.logical_not(opens))
        def _():
            base = jnp.where(row == 0, base_lists[0][8], base_lists[1][8])
            tile(rows_ref, even_ref, best_ref, limit_ref, row, base)

    @pl.when(opens)
    def _():
        arrive(8)

    meet_last(1 - core)

    @pl.when(plane == 0)
    def _():
        for slot in (1, 2):
            arrive(slot)

    def row_tops(row):
        return jnp.max(jnp.transpose(best_ref[pl.ds(row * count, count), :]), 0, keepdims=True)

    cols_ref[9] = row_tops(1 - core)
    back(9, 5, sibling).start()
    meet_last(core)
    top = jnp.maximum(row_tops(core), cols_ref[0])
    for slot in range(1, 10):
        pieces[slot].wait_send()

    @pl.when(core == 0)
    def _():
        for copy in heads_even.values():
            copy.wait_send()

    @pl.when(core == 1)
    def _():
        for copy in list(heads_odd.values()) + relays:
            copy.wait_send()

    back(9, 0, sibling).wait_send()

    @pl.when(jnp.logical_not(closes))
    def _():
        for slot in (4, 5, 6):
            back(slot, 0, sibling).wait_send()

    @pl.when(plane != 0)
    def _():
        for slot in (1, 2):
            back(slot, 0, sibling).wait_send()

    for slot, silent in ((3, planes - 1), (4, 1)):

        @pl.when(plane == silent)
        def _():
            got_ref[slot] = jnp.full((1, count), LOW, jnp.float32)

        @pl.when(plane != silent)
        def _():
            back(0, slot, sibling).wait_recv()

    back(0, 5, sibling).wait_recv()

    @pl.when(opens)
    def _():
        for slot in range(3):
            got_ref[slot] = jnp.full((1, count), LOW, jnp.float32)

    @pl.when(jnp.logical_not(opens))
    def _():
        for slot in range(3):
            back(0, slot, sibling).wait_recv()

    for slot in range(6):
        top = jnp.maximum(top, got_ref[slot])
    out_ref[...] = 1.0 - top * (1.0 / width)


def on_device(blocks, groups, series, tail, excl, band):
    count = series.shape[0]
    width = tail.shape[0] + 1
    hbm = pl.BlockSpec(memory_space=pltpu.HBM)
    window_cols = pltpu.VMEM((4 * width, count), jnp.bfloat16)
    out = pl.pallas_call(
        functools.partial(kernel, blocks, groups, width),
        out_shape=jax.ShapeDtypeStruct((1, count), jnp.float32),
        in_specs=[hbm, hbm, hbm, hbm],
        out_specs=pl.BlockSpec(memory_space=pltpu.VMEM),
        scratch_shapes=[
            pltpu.VMEM((1, count), jnp.float32),
            pltpu.VMEM((1, width - 1), jnp.float32),
            pltpu.VMEM((1, LANES), jnp.float32),
            pltpu.SMEM((1,), jnp.int32),
            pltpu.SMEM((1,), jnp.int32),
            pltpu.VMEM((10, 1, count + LANES), jnp.float32),
            pltpu.VMEM((2 * count, 4 * width), jnp.bfloat16),
            window_cols,
            window_cols,
            pltpu.VMEM((2 * count, LANES), jnp.float32),
            pltpu.VMEM((38 * count // SUBS, SUBS, LANES), jnp.float32),
            pltpu.VMEM((10, 1, count), jnp.float32),
            pltpu.VMEM((6, 1, count), jnp.float32),
            pltpu.SemaphoreType.DMA((4,)),
            pltpu.SemaphoreType.DMA((22,)),
            pltpu.SemaphoreType.DMA((10,)),
            pltpu.SemaphoreType.DMA((10,)),
            pltpu.SemaphoreType.DMA((10,)),
            pltpu.SemaphoreType.DMA((6,)),
            pltpu.SemaphoreType.REGULAR,
            pltpu.SemaphoreType.REGULAR,
        ],
        compiler_params=pltpu.CompilerParams(
            collective_id=0, has_side_effects=True, vmem_limit_bytes=48 * 1024 * 1024
        ),
    )(series.reshape(1, count), pltpu.with_memory_space_constraint(tail.reshape(1, width - 1), pltpu.HBM), excl, band)
    return out.reshape(count)


def solution(mesh):
    placed = (P(("blk", "merge")), P(), P(), P())
    body = functools.partial(on_device, mesh.shape["blk"], mesh.shape["merge"])
    return jax.shard_map(
        body, mesh=mesh, in_specs=placed, out_specs=P(("blk", "merge")), check_vma=False
    )
```
